128 devices in a mesh: dp: 4 (over y_hi, core), ctx: 32 (over x, y_lo, z).
Axes of the slice: x: 4, y: 4 (y_hi: 2, y_lo: 2; y = y_hi * 2 + y_lo), z: 4, core: 2. Of those that a mesh axis runs over, the one named last changes fastest.
Arguments:
- frames: float32 [4, 5120, 1536], P('dp', 'ctx'), may hold values from -6 to 6
- teacher: float32 [4, 1536, 768], P('dp'), may hold values from -0.4082483 to 0.4082483
- student: float32 [4, 1536, 768], P('dp'), may hold values from -0.4082483 to 0.4082483
- decay: float32 [4], P('dp'), may hold values from 0.3 to 0.8
- conv_weight: float32 [16, 96, 1536], replicated, may hold values from -0.15625 to 0.15625
- norm_gain: float32 [1536], replicated, may hold values from 0.1 to 1.9
Outputs:
- layer_out: float32 [4, 5120, 1536], P('dp', 'ctx')
- refreshed: float32 [4, 1536, 768], P('dp')
The draws below stay inside these ranges and needn't reach their ends.
All inputs are finite; a program needn't handle non-finite values.
Results may differ from the reference program's by a relative error of at most 0.0003.
Values sent between devices are 32-bit elements; how exact they have to be, the bound alone decides.
No kernel may reach another device: no remote copies, remote signals or barrier semaphores. Data moves between devices by JAX's collectives and lax.ppermute only.
A program may use at most 256 MiB of HBM per device.

```python
import jax
import jax.numpy as jnp
from jax import lax

D = 1536
HEADS = 12
HEAD_DIM = 64
GROUP_CH = 96
KERNEL = 16
FRAMES = 5120
RECS = 4


def projection_stack(key):
    subkeys = jax.random.split(key, 4)
    shape = (D, HEADS * HEAD_DIM)
    scale = D ** (-0.5)
    query_part = jax.random.truncated_normal(subkeys[0], -4.0, 4.0, shape, jnp.float32) * scale * 2.2
    key_part = jax.random.truncated_normal(subkeys[1], -4.0, 4.0, shape, jnp.float32) * scale * 2.2
    value_part = jax.random.truncated_normal(subkeys[2], -4.0, 4.0, shape, jnp.float32) * scale * 3.0
    out_part = jax.random.truncated_normal(subkeys[3], -4.0, 4.0, shape, jnp.float32) * scale * 3.0
    stacked = jnp.stack([query_part, key_part, value_part, out_part])
    return jnp.clip(stacked, -16.0 * scale, 16.0 * scale)


def draw_teacher(key, part):
    key = jax.random.fold_in(key, 11)
    return projection_stack(key)


def draw_student(key, part):
    key = jax.random.fold_in(key, 12)
    return projection_stack(key)


def steps_of(stream_key, dims, cuts, smallest, largest):
    gain = 1.0
    for dim, shards_of in cuts:
        steps = jax.random.uniform(jax.random.fold_in(jax.random.fold_in(stream_key, 6), dim), (shards_of,), jnp.float32, smallest / len(cuts), largest / len(cuts))
        gain = gain * jnp.repeat(jnp.exp(steps), dims[dim] // shards_of).reshape((-1,) + (1,) * (len(dims) - 1 - dim))
    return gain


def scatter_about(rng, shape, deviation, most, cuts=(), held_as=jnp.bfloat16):
    array = deviation * jax.random.normal(rng, shape, jnp.float32)
    if cuts:
        array = array * steps_of(rng, shape, cuts, -0.22, 0.18)
    return jnp.clip(array, -most, most).astype(held_as)


def setup_inputs(seed: int = 0) -> dict:
    seeds = jax.random.split(jax.random.key(seed), 7)
    frames = scatter_about(seeds[0], (RECS, FRAMES, D), 1.0, 6.0, ((0, 4), (1, 32)), jnp.float32)
    teacher = draw_teacher(jax.random.fold_in(seeds[6], 71), 0)
    student = draw_student(jax.random.fold_in(seeds[6], 71), 0)
    decay = jnp.clip(0.3 + 0.5 * jax.random.uniform(seeds[3], (4,), jnp.float32) ** steps_of(seeds[3], (4,), ((0, 4),), -0.2, 0.2), 0.3, 0.8)
    conv_weight = scatter_about(seeds[4], (KERNEL, GROUP_CH, D), (GROUP_CH * KERNEL) ** -0.5, 0.15625, (), jnp.float32)
    norm_gain = jnp.clip(1.0 + 0.18 * jax.random.normal(seeds[5], (D,), jnp.float32), 0.1, 1.9)
    return dict(frames=frames, teacher=teacher, student=student, decay=decay, conv_weight=conv_weight, norm_gain=norm_gain)


HIGH = lax.Precision.HIGHEST

def attend_recording(normed_rec, proj_query, proj_key, proj_value, proj_out):
    queries = jnp.dot(normed_rec, proj_query, precision=HIGH)
    key_rows = jnp.dot(normed_rec, proj_key, precision=HIGH)
    value_rows = jnp.dot(normed_rec, proj_value, precision=HIGH)
    query_heads = queries.reshape(FRAMES, HEADS, HEAD_DIM).transpose(1, 0, 2)
    key_heads = key_rows.reshape(FRAMES, HEADS, HEAD_DIM).transpose(1, 0, 2)
    value_heads = value_rows.reshape(FRAMES, HEADS, HEAD_DIM).transpose(1, 0, 2)

    def one_head(operands):
        query_one, key_one, value_one = operands
        scores = jnp.dot(query_one, key_one.T, precision=HIGH) * HEAD_DIM ** (-0.5)
        weights = jax.nn.softmax(scores, axis=-1)
        return jnp.dot(weights, value_one, precision=HIGH)
    per_head = lax.map(one_head, (query_heads, key_heads, value_heads))
    attended = per_head.transpose(1, 0, 2).reshape(FRAMES, HEADS * HEAD_DIM)
    return jnp.dot(attended, proj_out.T, precision=HIGH)

def reference(frames, teacher, student, decay, conv_weight, norm_gain):
    rates = decay[:, None, None]
    refreshed = rates * teacher + (1.0 - rates) * student
    reach = KERNEL // 2
    padded = jnp.pad(frames, ((0, 0), (reach, reach), (0, 0)))
    conv_out = lax.conv_general_dilated(padded, conv_weight, (1,), 'VALID', dimension_numbers=('NWC', 'WIO', 'NWC'), feature_group_count=D // GROUP_CH, precision=HIGH)[:, :FRAMES]
    mixed = frames + jax.nn.gelu(conv_out, approximate=False)
    center = lax.optimization_barrier(jnp.mean(mixed, axis=-1, keepdims=True))
    spread = lax.optimization_barrier(jnp.mean((mixed - center) ** 2, axis=-1, keepdims=True))
    normed = (mixed - center) / jnp.sqrt(spread + 1e-05) * norm_gain
    attended = lax.map(lambda rec: attend_recording(rec, refreshed[0], refreshed[1], refreshed[2], refreshed[3]), normed)
    return (mixed + attended, refreshed)
```

```python
import functools

import jax
import jax.numpy as jnp
from jax import lax
from jax.experimental import pallas as pl
from jax.experimental.pallas import tpu as pltpu
from jax.sharding import PartitionSpec as P

D = 1536
HEADS = 12
HEAD_DIM = 64
GROUP_CH = 96
KERNEL = 16
REACH = KERNEL // 2
ROWS = 160
QUAD = 4
COLS = HEADS * HEAD_DIM // QUAD
LOCAL_HEADS = HEADS // QUAD
HALF = D // 2
PACK = 2 * COLS
SPAN = QUAD * ROWS
LOG2E = 1.4426950408889634
MIB = 1 << 20
F32 = jnp.float32
BF16 = jnp.bfloat16
L_AT = HEAD_DIM
M_AT = HEAD_DIM + 1


def params(mib):
    return pltpu.CompilerParams(vmem_limit_bytes=mib * MIB)


def two_terms(value):
    high = value.astype(BF16)
    return high, (value - high.astype(F32)).astype(BF16)


def mm(a, b):
    return jnp.dot(a, b, preferred_element_type=F32)


def mm_nt(a, b):
    return lax.dot_general(a, b, (((1,), (1,)), ((), ())), preferred_element_type=F32)


def refresh_kernel(place, decay, teacher, student, refreshed, part):
    rate = decay[0]
    value = rate * teacher[...] + (1.0 - rate) * student[...]
    refreshed[...] = value
    for g in range(QUAD):
        @pl.when(place[1] == g)
        def _():
            cut = slice(g * COLS, (g + 1) * COLS)
            part[...] = jnp.concatenate([value[0, :, cut], value[1, :, cut]], axis=1)


def refresh(place, decay, teacher, student):
    step = 192
    block = pl.BlockSpec((2, step, 768), lambda i: (0, i, 0))
    smem = pl.BlockSpec(memory_space=pltpu.SMEM)
    refreshed, part = pl.pallas_call(
        refresh_kernel,
        grid=(HALF // step,),
        in_specs=[smem, smem, block, block],
        out_specs=[block, pl.BlockSpec((step, PACK), lambda i: (i, 0))],
        out_shape=[
            jax.ShapeDtypeStruct((2, HALF, 768), F32),
            jax.ShapeDtypeStruct((HALF, PACK), F32),
        ],
        compiler_params=params(24),
        cost_estimate=pl.CostEstimate(flops=4 * D * 768, bytes_accessed=15 * MIB, transcendentals=0),
        name="refresh",
    )(place, decay, teacher.reshape(2, HALF, 768), student.reshape(2, HALF, 768))
    return refreshed.reshape(1, D, 768), part


CONV_COLS = 4 * GROUP_CH


def conv_kernel(x, left, right, weight, gain, mixed, normed, padded, group, taps, rhs):
    step = pl.program_id(0)

    @pl.when(step == 0)
    def _():
        rhs[...] = jnp.zeros_like(rhs)

    padded[0:REACH, :] = left[...]
    padded[REACH:REACH + ROWS, :] = x[...]
    padded[REACH + ROWS:, :] = right[...]
    outs = []
    for q in range(4):
        cut = slice(q * GROUP_CH, (q + 1) * GROUP_CH)
        group[...] = jnp.concatenate(
            [padded[:, cut], jnp.zeros((ROWS + 2 * REACH, 128 - GROUP_CH), F32)], axis=1
        )
        for j in range(KERNEL):
            high, low = two_terms(group[j:j + ROWS, :])
            taps[:, j * 256:j * 256 + 128] = high
            taps[:, j * 256 + 128:j * 256 + 256] = low
            wide = jnp.concatenate(
                [weight[j, :, cut], jnp.zeros((GROUP_CH, 128 - GROUP_CH), F32)], axis=1
            )
            high, low = two_terms(wide)
            for base in (j * 256, j * 256 + 128):
                rhs[base:base + GROUP_CH, 0:128] = high
                rhs[base:base + GROUP_CH, 128:256] = low
        both = mm(taps[...], rhs[...])
        outs.append((both[:, :128] + both[:, 128:])[:, :GROUP_CH])
    conv = jnp.concatenate(outs, axis=1)
    value = x[...] + 0.5 * conv * (1.0 + lax.erf(conv * (0.5 ** 0.5)))
    for s in range(D // CONV_COLS):
        @pl.when(step == s)
        def _():
            mixed[:, s * CONV_COLS:(s + 1) * CONV_COLS] = value

    @pl.when(step == D // CONV_COLS - 1)
    def _():
        whole = mixed[...]
        center = jnp.sum(whole, axis=1, keepdims=True) * (1.0 / D)
        shifted = whole - center
        spread = jnp.sum(shifted * shifted, axis=1, keepdims=True) * (1.0 / D)
        normed[...] = shifted * (1.0 / jnp.sqrt(spread + 1e-5)) * gain[...]


def conv_norm(frames, left, right, weight, gain):
    whole = pl.BlockSpec((ROWS, D), lambda i: (0, 0))
    edge = pl.BlockSpec((REACH, CONV_COLS), lambda i: (0, i))
    return pl.pallas_call(
        conv_kernel,
        grid=(D // CONV_COLS,),
        in_specs=[
            pl.BlockSpec((ROWS, CONV_COLS), lambda i: (0, i)),
            edge,
            edge,
            pl.BlockSpec((KERNEL, GROUP_CH, CONV_COLS), lambda i: (0, 0, i)),
            pl.BlockSpec((1, D), lambda i: (0, 0)),
        ],
        out_specs=[whole, whole],
        out_shape=[jax.ShapeDtypeStruct((ROWS, D), F32)] * 2,
        scratch_shapes=[
            pltpu.VMEM((ROWS + 2 * REACH, CONV_COLS), F32),
            pltpu.VMEM((ROWS + 2 * REACH, 128), F32),
            pltpu.VMEM((ROWS, KERNEL * 256), BF16),
            pltpu.VMEM((KERNEL * 256, 256), BF16),
        ],
        compiler_params=params(40),
        cost_estimate=pl.CostEstimate(flops=10 * 10**9, bytes_accessed=12 * MIB, transcendentals=ROWS * D),
        name="conv_norm",
    )(frames, left, right, weight, gain)


def sort_kernel(place, own, core, cross, both, high, low, out_part):
    dp = place[0]
    parts = (own[...], core[...], cross[...], both[...])

    def tensor(t):
        which = jnp.bitwise_xor(dp, t)
        return jnp.where(
            which == 0, parts[0], jnp.where(which == 1, parts[1], jnp.where(which == 2, parts[2], parts[3]))
        )

    query, key, value = tensor(0), tensor(1), tensor(2)
    out_part[...] = tensor(3)
    gap = jnp.zeros((query.shape[0], 256 - COLS), F32)
    for half in range(2):
        cut = slice(half * COLS, (half + 1) * COLS)
        wide = jnp.concatenate([query[:, cut], gap, key[:, cut], value[:, cut]], axis=1)
        high[half], low[half] = two_terms(wide)


def sort_parts(place, own, core, cross, both):
    step = 96
    block = pl.BlockSpec((step, PACK), lambda i: (i, 0))
    wide = pl.BlockSpec((2, step, 256 + PACK), lambda i: (0, i, 0))
    high, low, out_part = pl.pallas_call(
        sort_kernel,
        grid=(HALF // step,),
        in_specs=[pl.BlockSpec(memory_space=pltpu.SMEM)] + [block] * 4,
        out_specs=[wide, wide, block],
        out_shape=[jax.ShapeDtypeStruct((2, HALF, 256 + PACK), BF16)] * 2
        + [jax.ShapeDtypeStruct((HALF, PACK), F32)],
        compiler_params=params(24),
        cost_estimate=pl.CostEstimate(flops=10**7, bytes_accessed=10 * MIB, transcendentals=0),
        name="sort_parts",
    )(place, own, core, cross, both)
    return high.reshape(D, 256 + PACK), low.reshape(D, 256 + PACK), out_part


def project_kernel(own, left, right, far_a, far_b, high, low, queries, pairs):
    def product(rows):
        rows_high, rows_low = two_terms(rows[...])
        return mm(rows_high, high[...]) + mm(rows_high, low[...]) + mm(rows_low, high[...])

    scale = HEAD_DIM ** (-0.5) * LOG2E
    first = product(own)
    pairs[0:ROWS, :] = first[:, 256:]
    second = product(left)
    pairs[ROWS:2 * ROWS, :] = second[:, 256:]
    third = product(right)
    pairs[2 * ROWS:3 * ROWS, :] = third[:, 256:]
    queries[0:ROWS, :] = jnp.concatenate([first[:, :COLS], third[:, :COLS]], axis=1) * scale
    half = ROWS // 2
    for part, far in enumerate((far_a, far_b)):
        last = product(far)
        at = 3 * ROWS + part * half
        pairs[at:at + half, :] = last[:, 256:]
        at = ROWS + part * half
        queries[at:at + half, :] = (
            jnp.concatenate([second[part * half:(part + 1) * half, :COLS], last[:, :COLS]], axis=1) * scale
        )


def project(own, left, right, far_a, far_b, high, low):
    return pl.pallas_call(
        project_kernel,
        out_shape=[
            jax.ShapeDtypeStruct((SPAN // 2, PACK), F32),
            jax.ShapeDtypeStruct((SPAN, PACK), F32),
        ],
        compiler_params=params(40),
        cost_estimate=pl.CostEstimate(flops=6 * SPAN * D * 640, bytes_accessed=10 * MIB, transcendentals=0),
        name="project",
    )(own, left, right, far_a, far_b, high, low)


def doubled(tile, odd):
    lane = lax.broadcasted_iota(jnp.int32, tile.shape, 1)
    turned = pltpu.roll(tile, 64, 1)
    return jnp.where((lane < 64) == (odd == 0), tile, turned)


def chunk(ref, rows, c):
    tile = ref[rows, (c // 2) * 128:(c // 2) * 128 + 128]
    return doubled(tile, c % 2)


def attend_kernel(n_queries, n_blocks, has_state, tile_rows, *refs):
    refs = list(refs)
    query_refs = [refs.pop(0) for _ in range(n_queries)]
    block_refs = [refs.pop(0) for _ in range(n_blocks)]
    state_in = refs.pop(0) if has_state else None
    state, query_cat, key_cat, value_cat = refs
    for n, ref in enumerate(query_refs):
        for half in range(2):
            at = n * SPAN + half * (SPAN // 2)
            for h in range(LOCAL_HEADS):
                value = chunk(ref, slice(None), half * LOCAL_HEADS + h)
                lane = lax.broadcasted_iota(jnp.int32, value.shape, 1)
                high = value.astype(BF16).astype(F32)
                mixture = jnp.where(lane < 64, high, value - high).astype(BF16)
                query_cat[h, at:at + SPAN // 2, 0:128] = mixture
                query_cat[h, at:at + SPAN // 2, 128:256] = mixture
    at = 0
    for ref in block_refs:
        count = ref.shape[0]
        for h in range(LOCAL_HEADS):
            high, low = two_terms(chunk(ref, slice(None), h))
            key_cat[h, at:at + count, 0:128] = high
            key_cat[h, at:at + count, 128:256] = low
            value = chunk(ref, slice(None), LOCAL_HEADS + h)
            lane = lax.broadcasted_iota(jnp.int32, value.shape, 1)
            high = value.astype(BF16).astype(F32)
            low = value - high
            high = jnp.where(lane < 64, high, jnp.where(lane == L_AT, 1.0, 0.0))
            value_cat[h, at:at + count, 0:128] = high.astype(BF16)
            value_cat[h, at:at + count, 128:256] = jnp.where(lane < 64, low, 0.0).astype(BF16)
        at += count
    tiles = n_queries * SPAN // tile_rows

    def body(i, _):
        h = i // tiles
        rows = pl.ds(pl.multiple_of((i % tiles) * tile_rows, tile_rows), tile_rows)
        scores = mm_nt(query_cat[h, rows, :], key_cat[h])
        top = jnp.max(scores, axis=1, keepdims=True)
        if has_state:
            before = state_in[h, rows, :]
            old = before[:, M_AT:M_AT + 1]
            top = jnp.maximum(top, old)
        probs = jnp.exp2(scores - top)
        high, low = two_terms(probs)
        both = mm(high, value_cat[h]) + mm(low, value_cat[h])
        after = both[:, :128] + both[:, 128:]
        if has_state:
            after = after + before * jnp.exp2(old - top)
        lane = lax.broadcasted_iota(jnp.int32, after.shape, 1)
        state[h, rows, :] = jnp.where(lane == M_AT, top, after)
        return 0

    lax.fori_loop(0, LOCAL_HEADS * tiles, body, 0)


def attend(queries, blocks, state=None, tile_rows=320):
    rows = SPAN * len(queries)
    keys = sum(b.shape[0] for b in blocks)
    shape = jax.ShapeDtypeStruct((LOCAL_HEADS, rows, 128), F32)
    operands = list(queries) + list(blocks) + ([] if state is None else [state])
    return pl.pallas_call(
        functools.partial(attend_kernel, len(queries), len(blocks), state is not None, tile_rows),
        out_shape=shape,
        scratch_shapes=[
            pltpu.VMEM((LOCAL_HEADS, rows, 256), BF16),
            pltpu.VMEM((LOCAL_HEADS, keys, 256), BF16),
            pltpu.VMEM((LOCAL_HEADS, keys, 256), BF16),
        ],
        compiler_params=params(48),
        cost_estimate=pl.CostEstimate(
            flops=2 * LOCAL_HEADS * rows * keys * 768, bytes_accessed=6 * MIB, transcendentals=LOCAL_HEADS * rows * keys
        ),
        name="attend",
    )(*operands)


def pack_kernel(state, packed):
    first, second, third = state[0], state[1], state[2]
    lane = lax.broadcasted_iota(jnp.int32, first.shape, 1)
    packed[:, 0:128] = jnp.where(lane < 64, first, pltpu.roll(second, 64, 1))
    packed[:, 128:256] = jnp.where(
        lane < 66, third, jnp.where(lane < 68, pltpu.roll(first, 2, 1), pltpu.roll(second, 4, 1))
    )


def pack(state):
    return pl.pallas_call(
        pack_kernel,
        out_shape=jax.ShapeDtypeStruct((SPAN, 256), F32),
        compiler_params=params(16),
        cost_estimate=pl.CostEstimate(flops=10**6, bytes_accessed=2 * MIB, transcendentals=0),
        name="pack",
    )(state)


def merge_kernel(state, packed, own, left, right, far):
    lane = lax.broadcasted_iota(jnp.int32, (SPAN, 128), 1)
    front, back = packed[:, 0:128], packed[:, 128:256]
    theirs = (
        (front, back[:, 66:67], back[:, 67:68]),
        (pltpu.roll(front, 64, 1), back[:, 68:69], back[:, 69:70]),
        (back, back[:, 64:65], back[:, 65:66]),
    )
    heads = []
    for h in range(LOCAL_HEADS):
        mine = state[h]
        other, other_sum, other_top = theirs[h]
        my_sum, my_top = mine[:, L_AT:L_AT + 1], mine[:, M_AT:M_AT + 1]
        top = jnp.maximum(my_top, other_top)
        a, b = jnp.exp2(my_top - top), jnp.exp2(other_top - top)
        share = 1.0 / (my_sum * a + other_sum * b)
        heads.append(mine * (a * share) + other * (b * share))
    tile = jnp.where(lane < 64, heads[0], pltpu.roll(heads[1], 64, 1))
    attended = jnp.concatenate([tile, heads[2][:, :64]], axis=1)
    half = ROWS // 2
    for s, ref in enumerate((own, left, right, far)):
        at = s * ROWS
        ref[...] = jnp.concatenate([attended[at:at + half], attended[at + half:at + ROWS]], axis=1)


def merge(state, packed):
    return pl.pallas_call(
        merge_kernel,
        out_shape=[jax.ShapeDtypeStruct((ROWS // 2, PACK), F32)] * 4,
        compiler_params=params(24),
        cost_estimate=pl.CostEstimate(flops=10**6, bytes_accessed=2 * MIB, transcendentals=0),
        name="merge",
    )(state, packed)


def output_kernel(mixed, own, left, right, far, part, part_left, part_right, part_far_a, part_far_b, out):
    total = [mixed[:, 0:HALF], mixed[:, HALF:D]]
    for att, parts in (
        (own, (part,)),
        (left, (part_left,)),
        (right, (part_right,)),
        (far, (part_far_a, part_far_b)),
    ):
        rows = jnp.concatenate([att[:, :COLS], att[:, COLS:]], axis=0)
        high, low = two_terms(rows)
        for half in range(2):
            cut = slice(half * COLS, (half + 1) * COLS)
            pieces = []
            for ref in parts:
                part_high, part_low = two_terms(ref[:, cut])
                pieces.append(mm_nt(high, part_high) + mm_nt(high, part_low) + mm_nt(low, part_high))
            total[half] = total[half] + (pieces[0] if len(pieces) == 1 else jnp.concatenate(pieces, axis=1))
    out[:, 0:HALF] = total[0]
    out[:, HALF:D] = total[1]


def output(*operands):
    return pl.pallas_call(
        output_kernel,
        out_shape=jax.ShapeDtypeStruct((ROWS, D), F32),
        compiler_params=params(40),
        cost_estimate=pl.CostEstimate(flops=6 * ROWS * 768 * D, bytes_accessed=8 * MIB, transcendentals=0),
        name="output",
    )(*operands)


def ctx_pairs(dx=0, dy=0, dz=0):
    return [
        ((x * 2 + y) * 4 + z, (((x + dx) % 4) * 2 + (y + dy) % 2) * 4 + (z + dz) % 4)
        for x in range(4)
        for y in range(2)
        for z in range(4)
    ]


def dp_pairs(flip_hi, flip_core):
    pairs = []
    for dp in range(4):
        for ctx in range(32):
            to_dp = dp ^ (2 * flip_hi + flip_core)
            to_ctx = ctx ^ 4 if flip_hi else ctx
            pairs.append((dp * 32 + ctx, to_dp * 32 + to_ctx))
    return pairs


def to_x(value, shift):
    return lax.ppermute(value, "ctx", ctx_pairs(dx=shift))


def to_z(value, shift):
    return lax.ppermute(value, "ctx", ctx_pairs(dz=shift))


def round_ring(move, block):
    before, after = move(block, 1), move(block, -1)
    half = block.shape[0] // 2
    far_a = move(after[:half], -1)
    far_b = move(before[half:], 1)
    return before, after, far_a, far_b


def local(frames, teacher, student, decay, conv_weight, norm_gain):
    dp, ctx = lax.axis_index("dp"), lax.axis_index("ctx")
    place = jnp.stack([dp, ctx // 8]).astype(jnp.int32)
    rows = frames[0]
    left = lax.ppermute(rows[ROWS - REACH:], "ctx", [(i, i + 1) for i in range(31)])
    right = lax.ppermute(rows[:REACH], "ctx", [(i + 1, i) for i in range(31)])

    refreshed, part = refresh(place, decay, teacher, student)
    cross = lax.ppermute(part, ("dp", "ctx"), dp_pairs(1, 0))
    core = lax.ppermute(part, ("dp", "ctx"), dp_pairs(0, 1))
    both = lax.ppermute(cross, ("dp", "ctx"), dp_pairs(0, 1))

    mixed, normed = conv_norm(rows, left, right, conv_weight, norm_gain.reshape(1, D))
    normed_blocks = round_ring(to_x, normed)

    high, low, out_part = sort_parts(place, part, core, cross, both)
    queries, pairs = project(normed, *normed_blocks, high, low)
    partner = lax.ppermute(queries, "ctx", ctx_pairs(dy=1))
    pair_before, pair_after, pair_far_a, pair_far_b = round_ring(to_z, pairs)
    out_blocks = round_ring(to_x, out_part)

    states = []
    for block in ((pairs,), (pair_before, pair_after)):
        states = [
            attend([q], block, None if not states else states[n]) for n, q in enumerate((partner, queries))
        ]
    theirs = attend([partner], (pair_far_a, pair_far_b), states[0])
    packed = lax.ppermute(pack(theirs), "ctx", ctx_pairs(dy=1))
    mine = attend([queries], (pair_far_a, pair_far_b), states[1])

    own, to_before, to_after, to_far = merge(mine, packed)
    from_after = to_x(to_before, -1)
    from_before = to_x(to_after, 1)
    from_far = to_x(to_far, 2)
    out = output(mixed, own, from_before, from_after, from_far, out_part, *out_blocks)
    return out[None], refreshed


def solution(mesh):
    return jax.shard_map(
        local,
        mesh=mesh,
        in_specs=(
            P("dp", "ctx", None),
            P("dp", None, None),
            P("dp", None, None),
            P("dp"),
            P(),
            P(),
        ),
        out_specs=(P("dp", "ctx", None), P("dp", None, None)),
        check_vma=False,
    )
```

```python
import functools

import jax
import jax.numpy as jnp
from jax import lax
from jax.experimental import pallas as pl
from jax.experimental.pallas import tpu as pltpu
from jax.sharding import PartitionSpec as P

D = 1536
HEADS = 12
HEAD_DIM = 64
GROUP_CH = 96
KERNEL = 16
REACH = KERNEL // 2
ROWS = 160
QUAD = 4
COLS = HEADS * HEAD_DIM // QUAD
LOCAL_HEADS = HEADS // QUAD
HALF = D // 2
PACK = 2 * COLS
SPAN = QUAD * ROWS
LOG2E = 1.4426950408889634
MIB = 1 << 20
F32 = jnp.float32
BF16 = jnp.bfloat16
L_AT = HEAD_DIM
M_AT = HEAD_DIM + 1


def params(mib):
    return pltpu.CompilerParams(vmem_limit_bytes=mib * MIB)


def two_terms(value):
    high = value.astype(BF16)
    return high, (value - high.astype(F32)).astype(BF16)


def mm(a, b):
    return jnp.dot(a, b, preferred_element_type=F32)


def mm_nt(a, b):
    return lax.dot_general(a, b, (((1,), (1,)), ((), ())), preferred_element_type=F32)


WINDOW = 256


PIECES = 4


def part_kernel(place, decay, frames, teacher, student, part, head, tail, old, new, sems):
    start = pl.multiple_of((3 * place[1] // 2) * 128, 128)
    step = HALF // PIECES
    copies = []
    for n, (src, dst) in enumerate(((teacher, old), (student, new))):
        for half in range(2):
            for piece in range(PIECES):
                rows = pl.ds(piece * step, step)
                copies.append(
                    pltpu.make_async_copy(
                        src.at[half, rows, pl.ds(start, WINDOW)], dst.at[half, rows, :], sems.at[n, half, piece]
                    )
                )
    for copy in copies:
        copy.start()
    head[...] = frames[0:REACH, :]
    tail[...] = frames[ROWS - REACH:, :]
    for copy in copies:
        copy.wait()
    rate = decay[0]
    odd = place[1] % 2
    for shift in range(2):
        @pl.when(odd == shift)
        def _():
            cut = slice(shift * 64, shift * 64 + COLS)
            halves = [rate * old[n, :, cut] + (1.0 - rate) * new[n, :, cut] for n in range(2)]
            part[...] = jnp.concatenate(halves, axis=1)


def head_part(place, decay, frames, teacher, student):
    smem = pl.BlockSpec(memory_space=pltpu.SMEM)
    hbm = pl.BlockSpec(memory_space=pltpu.HBM)
    return pl.pallas_call(
        part_kernel,
        in_specs=[smem, smem, pl.BlockSpec(memory_space=pltpu.VMEM), hbm, hbm],
        out_shape=[
            jax.ShapeDtypeStruct((HALF, PACK), F32),
            jax.ShapeDtypeStruct((REACH, D), F32),
            jax.ShapeDtypeStruct((REACH, D), F32),
        ],
        scratch_shapes=[
            pltpu.VMEM((2, HALF, WINDOW), F32),
            pltpu.VMEM((2, HALF, WINDOW), F32),
            pltpu.SemaphoreType.DMA((2, 2, PIECES)),
        ],
        compiler_params=params(56),
        cost_estimate=pl.CostEstimate(flops=4 * D * COLS, bytes_accessed=4 * MIB, transcendentals=0),
        name="head_part",
    )(place, decay, frames, teacher.reshape(2, HALF, 768), student.reshape(2, HALF, 768))


def refresh_kernel(decay, teacher, student, token, refreshed):
    rate = decay[0]
    refreshed[...] = rate * teacher[...] + (1.0 - rate) * student[...]


def refresh(decay, teacher, student, token):
    step = 384
    block = pl.BlockSpec((1, step, 768), lambda i: (0, i, 0))
    return pl.pallas_call(
        refresh_kernel,
        grid=(D // step,),
        in_specs=[pl.BlockSpec(memory_space=pltpu.SMEM), block, block, pl.BlockSpec(memory_space=pl.ANY)],
        out_specs=block,
        out_shape=jax.ShapeDtypeStruct((1, D, 768), F32),
        compiler_params=params(16),
        cost_estimate=pl.CostEstimate(flops=4 * D * 768, bytes_accessed=14 * MIB, transcendentals=0),
        name="refresh",
    )(decay, teacher, student, token)


def hold_kernel(value, token, out):
    out[...] = value[...]


def hold(value, token):
    return pl.pallas_call(
        hold_kernel,
        in_specs=[pl.BlockSpec(memory_space=pltpu.VMEM), pl.BlockSpec(memory_space=pl.ANY)],
        out_shape=jax.ShapeDtypeStruct(value.shape, F32),
        compiler_params=params(8),
        cost_estimate=pl.CostEstimate(flops=0, bytes_accessed=10**6, transcendentals=0),
        name="hold",
    )(value, token)


def duo_kernel(own, core, out):
    out[0] = own[...]
    out[1] = core[...]


def duo(own, core):
    return pl.pallas_call(
        duo_kernel,
        out_shape=jax.ShapeDtypeStruct((2, HALF, PACK), F32),
        compiler_params=params(16),
        cost_estimate=pl.CostEstimate(flops=0, bytes_accessed=10**6, transcendentals=0),
        name="duo",
    )(own, core)


CONV_COLS = 4 * GROUP_CH


def conv_kernel(x, left, right, weight, gain, token, mixed, top, bottom, padded, *scratch):
    groups, taps, rhs = scratch[0:2], scratch[2:4], scratch[4:6]
    step = pl.program_id(0)

    @pl.when(step == 0)
    def _():
        for ref in rhs:
            ref[...] = jnp.zeros_like(ref)

    padded[0:REACH, :] = left[...]
    padded[REACH:REACH + ROWS, :] = x[...]
    padded[REACH + ROWS:, :] = right[...]
    outs = []
    for q in range(4):
        cut = slice(q * GROUP_CH, (q + 1) * GROUP_CH)
        group, tap, part = groups[q % 2], taps[q % 2], rhs[q % 2]
        group[...] = jnp.concatenate(
            [padded[:, cut], jnp.zeros((ROWS + 2 * REACH, 128 - GROUP_CH), F32)], axis=1
        )
        for j in range(KERNEL):
            at = j * 128
            high, low = two_terms(group[j:j + ROWS, :])
            tap[0:ROWS, at:at + 128] = high
            tap[ROWS:, at:at + 128] = low
            wide = jnp.concatenate(
                [weight[j, :, cut], jnp.zeros((GROUP_CH, 128 - GROUP_CH), F32)], axis=1
            )
            high, low = two_terms(wide)
            part[at:at + GROUP_CH, 0:128] = high
            part[at:at + GROUP_CH, 128:256] = low
        both = mm(tap[...], part[...])
        both = both[:ROWS] + both[ROWS:]
        outs.append((both[:, :128] + both[:, 128:])[:, :GROUP_CH])
    conv = jnp.concatenate(outs, axis=1)
    value = x[...] + 0.5 * conv * (1.0 + lax.erf(conv * (0.5 ** 0.5)))
    for s in range(D // CONV_COLS):
        @pl.when(step == s)
        def _():
            mixed[:, s * CONV_COLS:(s + 1) * CONV_COLS] = value

    @pl.when(step == D // CONV_COLS - 1)
    def _():
        whole = mixed[...]
        center = jnp.sum(whole, axis=1, keepdims=True) * (1.0 / D)
        shifted = whole - center
        spread = jnp.sum(shifted * shifted, axis=1, keepdims=True) * (1.0 / D)
        normed = shifted * (1.0 / jnp.sqrt(spread + 1e-5)) * gain[...]
        top[...] = normed[:ROWS // 2]
        bottom[...] = normed[ROWS // 2:]


def conv_norm(frames, left, right, weight, gain, token):
    whole = pl.BlockSpec((ROWS, D), lambda i: (0, 0))
    half = pl.BlockSpec((ROWS // 2, D), lambda i: (0, 0))
    edge = pl.BlockSpec((REACH, CONV_COLS), lambda i: (0, i))
    return pl.pallas_call(
        conv_kernel,
        grid=(D // CONV_COLS,),
        in_specs=[
            pl.BlockSpec((ROWS, CONV_COLS), lambda i: (0, i)),
            edge,
            edge,
            pl.BlockSpec((KERNEL, GROUP_CH, CONV_COLS), lambda i: (0, 0, i)),
            pl.BlockSpec((1, D), lambda i: (0, 0)),
            pl.BlockSpec(memory_space=pl.ANY),
        ],
        out_specs=[whole, half, half],
        out_shape=[jax.ShapeDtypeStruct((ROWS, D), F32)] + [jax.ShapeDtypeStruct((ROWS // 2, D), F32)] * 2,
        scratch_shapes=[
            pltpu.VMEM((ROWS + 2 * REACH, CONV_COLS), F32),
        ]
        + [pltpu.VMEM((ROWS + 2 * REACH, 128), F32)] * 2
        + [pltpu.VMEM((2 * ROWS, KERNEL * 128), BF16)] * 2
        + [pltpu.VMEM((KERNEL * 128, 256), BF16)] * 2,
        compiler_params=params(56),
        cost_estimate=pl.CostEstimate(flops=10**6, bytes_accessed=10**6, transcendentals=0),
        name="conv_norm",
    )(frames, left, right, weight, gain, token)


def sort_kernel(place, own, core, cross, *refs):
    high, low, out_part, out_half = refs[-4:]
    dp = place[0]
    parts = (own[...], core[...], cross[0], cross[1])

    def tensor(t):
        which = jnp.bitwise_xor(dp, t)
        return jnp.where(
            which == 0, parts[0], jnp.where(which == 1, parts[1], jnp.where(which == 2, parts[2], parts[3]))
        )

    query, key, value = tensor(0), tensor(1), tensor(2)
    out_part[...] = tensor(3)
    turns = pl.num_programs(0) // 2

    @pl.when(pl.program_id(0) // turns == dp % 2)
    def _():
        out_half[pl.ds(pl.program_id(0) % turns * out_part.shape[0], out_part.shape[0]), :] = out_part[...]

    gap = jnp.zeros((query.shape[0], 256 - COLS), F32)
    for half in range(2):
        cut = slice(half * COLS, (half + 1) * COLS)
        wide = jnp.concatenate([query[:, cut], gap, key[:, cut], value[:, cut]], axis=1)
        high[half], low[half] = two_terms(wide)


def sort_parts(place, own, core, cross):
    step = 96
    block = pl.BlockSpec((step, PACK), lambda i: (i, 0))
    wide = pl.BlockSpec((2, step, 256 + PACK), lambda i: (0, i, 0))
    high, low, out_part, out_half = pl.pallas_call(
        sort_kernel,
        grid=(HALF // step,),
        in_specs=[pl.BlockSpec(memory_space=pltpu.SMEM)]
        + [block] * 2
        + [pl.BlockSpec((2, step, PACK), lambda i: (0, i, 0))],
        out_specs=[wide, wide, block, pl.BlockSpec((HALF // 2, PACK), lambda i: (0, 0))],
        out_shape=[jax.ShapeDtypeStruct((2, HALF, 256 + PACK), BF16)] * 2
        + [jax.ShapeDtypeStruct((HALF, PACK), F32), jax.ShapeDtypeStruct((HALF // 2, PACK), F32)],
        compiler_params=params(24),
        cost_estimate=pl.CostEstimate(flops=10**7, bytes_accessed=10 * MIB, transcendentals=0),
        name="sort_parts",
    )(place, own, core, cross)
    return high.reshape(D, 256 + PACK), low.reshape(D, 256 + PACK), out_part, out_half


def collect_kernel(before, after, far, token, out):
    for n, ref in enumerate((before, after, far)):
        out[n] = ref[...]


def collect(*operands):
    vmem = pl.BlockSpec(memory_space=pltpu.VMEM)
    return pl.pallas_call(
        collect_kernel,
        in_specs=[vmem] * 3 + [pl.BlockSpec(memory_space=pl.ANY)],
        out_shape=jax.ShapeDtypeStruct((QUAD - 1, HALF // 2, PACK), F32),
        compiler_params=params(8),
        cost_estimate=pl.CostEstimate(flops=10**6, bytes_accessed=10**6, transcendentals=0),
        name="collect",
    )(*operands)


def split_out_kernel(place, own, mine, other, high, low):
    here = pl.program_id(0) // (pl.num_programs(0) // 2) == place[0] % 2
    for g in range(QUAD):
        whole = own[...] if g == 0 else jnp.where(here, mine[g - 1], other[g - 1])
        for half in range(2):
            high[g, half], low[g, half] = two_terms(whole[:, half * COLS:(half + 1) * COLS])


def split_out(place, own, mine, other):
    step = 192
    turns = HALF // step // 2
    out = pl.BlockSpec((QUAD, 2, step, COLS), lambda i: (0, 0, i, 0))
    part = pl.BlockSpec((QUAD - 1, step, PACK), lambda i: (0, i % turns, 0))
    return pl.pallas_call(
        split_out_kernel,
        grid=(HALF // step,),
        in_specs=[
            pl.BlockSpec(memory_space=pltpu.SMEM),
            pl.BlockSpec((step, PACK), lambda i: (i, 0)),
            part,
            part,
        ],
        out_specs=[out, out],
        out_shape=[jax.ShapeDtypeStruct((QUAD, 2, HALF, COLS), BF16)] * 2,
        compiler_params=params(16),
        cost_estimate=pl.CostEstimate(flops=10**6, bytes_accessed=10**6, transcendentals=0),
        name="split_out",
    )(place, own, mine, other)


SCALE = HEAD_DIM ** (-0.5) * LOG2E
NEAR = 3 * ROWS
FAR = ROWS


def projected(rows, high, low):
    rows_high, rows_low = two_terms(rows)
    return mm(rows_high, high[...]) + mm(rows_high, low[...]) + mm(rows_low, high[...])


def project_cost(rows):
    return pl.CostEstimate(flops=6 * rows * D * 640, bytes_accessed=4 * MIB, transcendentals=0)


def project_near_kernel(*refs):
    high, low, queries, pairs = refs[-4:]
    values = []
    for n in range(3):
        rows = jnp.concatenate([refs[2 * n][...], refs[2 * n + 1][...]], axis=0)
        value = projected(rows, high, low)
        pairs[n * ROWS:(n + 1) * ROWS, :] = value[:, 256:]
        values.append(value[:, :COLS] * SCALE)
    half = ROWS // 2
    first, second, third = values
    queries[0:half, :] = jnp.concatenate([first[:half], second[half:]], axis=1)
    queries[half:ROWS, :] = jnp.concatenate([first[half:], third[:half]], axis=1)
    queries[ROWS:, :] = jnp.concatenate([second[:half], third[half:]], axis=1)


def project_near(*operands):
    return pl.pallas_call(
        project_near_kernel,
        out_shape=[jax.ShapeDtypeStruct((NEAR // 2, PACK), F32), jax.ShapeDtypeStruct((NEAR, PACK), F32)],
        compiler_params=params(24),
        cost_estimate=pl.CostEstimate(flops=6 * NEAR * D * 640, bytes_accessed=40 * MIB, transcendentals=0),
        name="project_near",
    )(*operands)


def project_far_kernel(far_a, far_b, near_queries, near_pairs, high, low, queries, pairs):
    half = ROWS // 2
    value = projected(jnp.concatenate([far_a[...], far_b[...]], axis=0), high, low)
    pairs[0:NEAR, :] = near_pairs[...]
    pairs[NEAR:, :] = value[:, 256:]
    value = value[:, :COLS] * SCALE
    queries[0:NEAR // 2, :] = near_queries[...]
    queries[NEAR // 2:, :] = jnp.concatenate([value[:half], value[half:]], axis=1)


def project_far(*operands):
    return pl.pallas_call(
        project_far_kernel,
        out_shape=[
            jax.ShapeDtypeStruct((SPAN // 2, PACK), F32),
            jax.ShapeDtypeStruct((SPAN, PACK), F32),
        ],
        compiler_params=params(24),
        cost_estimate=project_cost(ROWS),
        name="project_far",
    )(*operands)


def halves_kernel(before, after, token, first, second):
    half = SPAN // 2
    first[...] = after[0:half, :]
    second[...] = before[half:, :]


def halves(*operands):
    vmem = pl.BlockSpec(memory_space=pltpu.VMEM)
    return pl.pallas_call(
        halves_kernel,
        in_specs=[vmem] * 2 + [pl.BlockSpec(memory_space=pl.ANY)],
        out_shape=[jax.ShapeDtypeStruct((SPAN // 2, PACK), F32)] * 2,
        compiler_params=params(12),
        cost_estimate=pl.CostEstimate(flops=10**5, bytes_accessed=2 * MIB, transcendentals=0),
        name="halves",
    )(*operands)


def doubled(tile, odd):
    lane = lax.broadcasted_iota(jnp.int32, tile.shape, 1)
    turned = pltpu.roll(tile, 64, 1)
    return jnp.where((lane < 64) == (odd == 0), tile, turned)


def chunk(ref, c):
    return doubled(ref[:, (c // 2) * 128:(c // 2) * 128 + 128], c % 2)


def attend_kernel(n_queries, n_blocks, state_rows, has_token, *refs):
    refs = list(refs)
    query_refs = [refs.pop(0) for _ in range(n_queries)]
    block_refs = [refs.pop(0) for _ in range(n_blocks)]
    state_refs = [refs.pop(0) for _ in state_rows]
    if has_token:
        refs.pop(0)
    state, query_cat, key_cat, value_cat, even, odd = refs
    at = 0
    for ref in query_refs:
        count = ref.shape[0]
        for half in range(2):
            for h in range(LOCAL_HEADS):
                value = chunk(ref, half * LOCAL_HEADS + h)
                lane = lax.broadcasted_iota(jnp.int32, value.shape, 1)
                high = value.astype(BF16).astype(F32)
                mixture = jnp.where(lane < 64, high, value - high).astype(BF16)
                query_cat[h, at:at + count, 0:128] = mixture
                query_cat[h, at:at + count, 128:256] = mixture
            at += count
    at = 0
    for ref in block_refs:
        count = ref.shape[0]
        for h in range(LOCAL_HEADS):
            high, low = two_terms(chunk(ref, h))
            key_cat[h, at:at + count, 0:128] = high
            key_cat[h, at:at + count, 128:256] = low
            value = chunk(ref, LOCAL_HEADS + h)
            lane = lax.broadcasted_iota(jnp.int32, value.shape, 1)
            high = value.astype(BF16).astype(F32)
            low = value - high
            high = jnp.where(lane < 64, high, jnp.where(lane == L_AT, 1.0, 0.0))
            value_cat[h, at:at + count, 0:128] = high.astype(BF16)
            value_cat[h, at:at + count, 128:256] = jnp.where(lane < 64, low, 0.0).astype(BF16)
        at += count

    at = 0
    for ref, (row, count) in zip(state_refs, state_rows):
        state[:, at:at + count, :] = ref[:, row:row + count, :]
        at += count

    def place(i):
        return i % LOCAL_HEADS, i // LOCAL_HEADS * SPAN

    def scores(i):
        h, at = place(i)
        return mm_nt(query_cat[h, pl.ds(at, SPAN), :], key_cat[h])

    def finish(i, value):
        h, at = place(i)
        top = jnp.max(value, axis=1, keepdims=True)
        if state_rows:
            before = state[h, pl.ds(at, SPAN), :]
            old = before[:, M_AT:M_AT + 1]
            top = jnp.maximum(top, old)
        high, low = two_terms(jnp.exp2(value - top))
        both = mm(jnp.concatenate([high, low], axis=0), value_cat[h])
        both = both[:SPAN] + both[SPAN:]
        after = both[:, :128] + both[:, 128:]
        if state_rows:
            after = after + before * jnp.exp2(old - top)
        lane = lax.broadcasted_iota(jnp.int32, after.shape, 1)
        state[h, pl.ds(at, SPAN), :] = jnp.where(lane == M_AT, top, after)

    total = state.shape[1] // SPAN * LOCAL_HEADS
    even[...] = scores(0)

    def body(j, _):
        i = 2 * j
        odd[...] = scores(i + 1)
        finish(i, even[...])
        even[...] = scores(i + 2)
        finish(i + 1, odd[...])
        return 0

    pairs = (total - 1) // 2
    lax.fori_loop(0, pairs, body, 0)
    if total % 2 == 0:
        odd[...] = scores(total - 1)
        finish(total - 2, even[...])
        finish(total - 1, odd[...])
    else:
        finish(total - 1, even[...])


def attend(queries, blocks, states=(), state_rows=(), token=None, cost=1):
    rows = sum(2 * q.shape[0] for q in queries)
    keys = sum(b.shape[0] for b in blocks)
    shape = jax.ShapeDtypeStruct((LOCAL_HEADS, rows, 128), F32)
    operands = list(queries) + list(blocks) + list(states)
    specs = [pl.BlockSpec(memory_space=pltpu.VMEM)] * len(operands)
    if token is not None:
        operands.append(token)
        specs.append(pl.BlockSpec(memory_space=pl.ANY))
    return pl.pallas_call(
        functools.partial(attend_kernel, len(queries), len(blocks), state_rows, token is not None),
        in_specs=specs,
        out_shape=shape,
        scratch_shapes=[
            pltpu.VMEM((LOCAL_HEADS, rows, 256), BF16),
            pltpu.VMEM((LOCAL_HEADS, keys, 256), BF16),
            pltpu.VMEM((LOCAL_HEADS, keys, 256), BF16),
            pltpu.VMEM((SPAN, keys), F32),
            pltpu.VMEM((SPAN, keys), F32),
        ],
        compiler_params=params(44),
        cost_estimate=pl.CostEstimate(flops=cost * 10**6, bytes_accessed=cost * 10**6, transcendentals=0),
        name="attend",
    )(*operands)


def pack_kernel(state, packed):
    first, second, third = state[0], state[1], state[2]
    lane = lax.broadcasted_iota(jnp.int32, first.shape, 1)
    packed[:, 0:128] = jnp.where(lane < 64, first, pltpu.roll(second, 64, 1))
    packed[:, 128:256] = jnp.where(
        lane < 66, third, jnp.where(lane < 68, pltpu.roll(first, 2, 1), pltpu.roll(second, 4, 1))
    )


def pack(state):
    return pl.pallas_call(
        pack_kernel,
        out_shape=jax.ShapeDtypeStruct((SPAN, 256), F32),
        compiler_params=params(16),
        cost_estimate=pl.CostEstimate(flops=10**6, bytes_accessed=2 * MIB, transcendentals=0),
        name="pack",
    )(state)


def merge_kernel(state, packed, own, left, right, far):
    lane = lax.broadcasted_iota(jnp.int32, (SPAN, 128), 1)
    front, back = packed[:, 0:128], packed[:, 128:256]
    theirs = (
        (front, back[:, 66:67], back[:, 67:68]),
        (pltpu.roll(front, 64, 1), back[:, 68:69], back[:, 69:70]),
        (back, back[:, 64:65], back[:, 65:66]),
    )
    heads = []
    for h in range(LOCAL_HEADS):
        mine = state[h]
        other, other_sum, other_top = theirs[h]
        my_sum, my_top = mine[:, L_AT:L_AT + 1], mine[:, M_AT:M_AT + 1]
        top = jnp.maximum(my_top, other_top)
        a, b = jnp.exp2(my_top - top), jnp.exp2(other_top - top)
        share = 1.0 / (my_sum * a + other_sum * b)
        heads.append(mine * (a * share) + other * (b * share))
    tile = jnp.where(lane < 64, heads[0], pltpu.roll(heads[1], 64, 1))
    attended = jnp.concatenate([tile, heads[2][:, :64]], axis=1)
    half = ROWS // 2
    pieces = [attended[n * half:(n + 1) * half] for n in range(2 * QUAD)]
    for ref, (a, b) in ((own, (0, 1)), (left, (2, 4)), (right, (5, 6)), (far, (3, 7))):
        ref[...] = jnp.concatenate([pieces[a], pieces[b]], axis=1)


def merge(state, packed):
    return pl.pallas_call(
        merge_kernel,
        out_shape=[jax.ShapeDtypeStruct((ROWS // 2, PACK), F32)] * 4,
        compiler_params=params(24),
        cost_estimate=pl.CostEstimate(flops=10**6, bytes_accessed=2 * MIB, transcendentals=0),
        name="merge",
    )(state, packed)


def output_kernel(mixed, own, before, after, far, high, low, out):
    terms = [two_terms(jnp.concatenate([ref[:, :COLS], ref[:, COLS:]], axis=0)) for ref in (own, before, after, far)]
    for half in range(2):
        cut = slice(half * HALF, (half + 1) * HALF)
        total = mixed[:, cut]
        for g, (rows_high, rows_low) in enumerate(terms):
            total = total + (
                mm_nt(rows_high, high[g, half])
                + mm_nt(rows_high, low[g, half])
                + mm_nt(rows_low, high[g, half])
            )
        out[:, cut] = total


def output(*operands):
    return pl.pallas_call(
        output_kernel,
        out_shape=jax.ShapeDtypeStruct((ROWS, D), F32),
        compiler_params=params(32),
        cost_estimate=pl.CostEstimate(flops=6 * ROWS * 768 * D, bytes_accessed=8 * MIB, transcendentals=0),
        name="output",
    )(*operands)


def ctx_pairs(dx=0, dy=0, dz=0):
    return [
        ((x * 2 + y) * 4 + z, (((x + dx) % 4) * 2 + (y + dy) % 2) * 4 + (z + dz) % 4)
        for x in range(4)
        for y in range(2)
        for z in range(4)
    ]


def dp_pairs(flip_hi, flip_core):
    pairs = []
    for dp in range(4):
        for ctx in range(32):
            to_dp = dp ^ (2 * flip_hi + flip_core)
            to_ctx = ctx ^ 4 if flip_hi else ctx
            pairs.append((dp * 32 + ctx, to_dp * 32 + to_ctx))
    return pairs


def to_x(value, shift):
    return lax.ppermute(value, "ctx", ctx_pairs(dx=shift))


def to_y(value):
    return lax.ppermute(value, "ctx", ctx_pairs(dy=1))


def to_z(value, shift):
    return lax.ppermute(value, "ctx", ctx_pairs(dz=shift))


def local(frames, teacher, student, decay, conv_weight, norm_gain):
    dp, ctx = lax.axis_index("dp"), lax.axis_index("ctx")
    place = jnp.stack([dp, ctx // 8]).astype(jnp.int32)
    rows = frames[0]
    part, head, tail = head_part(place, decay, rows, teacher, student)
    left = lax.ppermute(tail, "ctx", [(i, i + 1) for i in range(31)])
    right = lax.ppermute(head, "ctx", [(i + 1, i) for i in range(31)])

    core = lax.ppermute(part, ("dp", "ctx"), dp_pairs(0, 1))
    both = duo(part, core)
    cross = lax.ppermute(both, ("dp", "ctx"), dp_pairs(1, 0))

    mixed, top, bottom = conv_norm(rows, left, right, conv_weight, norm_gain.reshape(1, D), both)
    after_top, before_bottom = to_x(top, -1), to_x(bottom, 1)
    far_a, far_b = to_x(after_top, -1), to_x(before_bottom, 1)
    after_bottom, before_top = to_x(bottom, -1), to_x(top, 1)
    refreshed = refresh(decay, teacher, student, top)
    high, low, out_part, out_half = sort_parts(place, part, core, cross)
    near_queries, near_pairs = project_near(
        top, bottom, before_top, before_bottom, after_top, after_bottom, high, low
    )
    mine, pairs = project_far(far_a, far_b, near_queries, near_pairs, high, low)
    partner = to_y(mine)
    around = [to_z(pairs, 1), to_z(pairs, -1)]

    all_rows = (0, SPAN)
    ours = attend([mine], [pairs])
    theirs = attend([partner], [pairs], token=ours)
    out_half = hold(out_half, theirs)
    out_halves = [to_x(out_half, 1), to_x(out_half, -1), to_x(out_half, 2)]
    first, second = halves(*around, theirs)
    opposite = [to_z(first, -1), to_z(second, 1)]
    theirs = attend([partner], around, [theirs], (all_rows,), first, cost=20)
    theirs = attend([partner], opposite, [theirs], (all_rows,))
    sums = pack(theirs)
    packed = to_y(sums)
    ours = attend([mine], around + opposite, [ours], (all_rows,), sums)
    own, to_before, to_after, to_far = merge(ours, packed)
    collected = collect(*out_halves, sums)
    other = lax.ppermute(collected, ("dp", "ctx"), dp_pairs(0, 1))
    out_high, out_low = split_out(place, out_part, collected, other)

    from_after = to_x(to_before, -1)
    from_before = to_x(to_after, 1)
    from_far = to_x(to_far, 2)
    out = output(mixed, own, from_before, from_after, from_far, out_high, out_low)
    return out[None], refreshed


def solution(mesh):
    return jax.shard_map(
        local,
        mesh=mesh,
        in_specs=(
            P("dp", "ctx", None),
            P("dp", None, None),
            P("dp", None, None),
            P("dp"),
            P(),
            P(),
        ),
        out_specs=(P("dp", "ctx", None), P("dp", None, None)),
        check_vma=False,
    )
```

```python
import functools

import jax
import jax.numpy as jnp
from jax import lax
from jax.experimental import pallas as pl
from jax.experimental.pallas import tpu as pltpu
from jax.sharding import PartitionSpec as P

D = 1536
HEADS = 12
HEAD_DIM = 64
GROUP_CH = 96
KERNEL = 16
REACH = KERNEL // 2
ROWS = 160
QUAD = 4
COLS = HEADS * HEAD_DIM // QUAD
LOCAL_HEADS = HEADS // QUAD
HALF = D // 2
PACK = 2 * COLS
SPAN = QUAD * ROWS
LOG2E = 1.4426950408889634
MIB = 1 << 20
F32 = jnp.float32
BF16 = jnp.bfloat16
L_AT = HEAD_DIM
M_AT = HEAD_DIM + 1


def params(mib):
    return pltpu.CompilerParams(vmem_limit_bytes=mib * MIB)


def two_terms(value):
    high = value.astype(BF16)
    return high, (value - high.astype(F32)).astype(BF16)


def mm(a, b):
    return jnp.dot(a, b, preferred_element_type=F32)


def mm_nt(a, b):
    return lax.dot_general(a, b, (((1,), (1,)), ((), ())), preferred_element_type=F32)


WINDOW = 256


PIECES = 4


def part_kernel(place, decay, frames, teacher, student, part, head, tail, old, new, sems):
    start = pl.multiple_of((3 * place[1] // 2) * 128, 128)
    step = HALF // PIECES
    copies = []
    for n, (src, dst) in enumerate(((teacher, old), (student, new))):
        for half in range(2):
            for piece in range(PIECES):
                rows = pl.ds(piece * step, step)
                copies.append(
                    pltpu.make_async_copy(
                        src.at[half, rows, pl.ds(start, WINDOW)], dst.at[half, rows, :], sems.at[n, half, piece]
                    )
                )
    for copy in copies:
        copy.start()
    head[...] = frames[0:REACH, :]
    tail[...] = frames[ROWS - REACH:, :]
    for copy in copies:
        copy.wait()
    rate = decay[0]
    odd = place[1] % 2
    for shift in range(2):
        @pl.when(odd == shift)
        def _():
            cut = slice(shift * 64, shift * 64 + COLS)
            halves = [rate * old[n, :, cut] + (1.0 - rate) * new[n, :, cut] for n in range(2)]
            part[...] = jnp.concatenate(halves, axis=1)


def head_part(place, decay, frames, teacher, student):
    smem = pl.BlockSpec(memory_space=pltpu.SMEM)
    hbm = pl.BlockSpec(memory_space=pltpu.HBM)
    return pl.pallas_call(
        part_kernel,
        in_specs=[smem, smem, pl.BlockSpec(memory_space=pltpu.VMEM), hbm, hbm],
        out_shape=[
            jax.ShapeDtypeStruct((HALF, PACK), F32),
            jax.ShapeDtypeStruct((REACH, D), F32),
            jax.ShapeDtypeStruct((REACH, D), F32),
        ],
        scratch_shapes=[
            pltpu.VMEM((2, HALF, WINDOW), F32),
            pltpu.VMEM((2, HALF, WINDOW), F32),
            pltpu.SemaphoreType.DMA((2, 2, PIECES)),
        ],
        compiler_params=params(56),
        cost_estimate=pl.CostEstimate(flops=4 * D * COLS, bytes_accessed=4 * MIB, transcendentals=0),
        name="head_part",
    )(place, decay, frames, teacher.reshape(2, HALF, 768), student.reshape(2, HALF, 768))


def refresh_kernel(decay, teacher, student, token, refreshed):
    rate = decay[0]
    refreshed[...] = rate * teacher[...] + (1.0 - rate) * student[...]


def refresh(decay, teacher, student, token):
    step = 384
    block = pl.BlockSpec((1, step, 768), lambda i: (0, i, 0))
    return pl.pallas_call(
        refresh_kernel,
        grid=(D // step,),
        in_specs=[pl.BlockSpec(memory_space=pltpu.SMEM), block, block, pl.BlockSpec(memory_space=pl.ANY)],
        out_specs=block,
        out_shape=jax.ShapeDtypeStruct((1, D, 768), F32),
        compiler_params=params(16),
        cost_estimate=pl.CostEstimate(flops=4 * D * 768, bytes_accessed=14 * MIB, transcendentals=0),
        name="refresh",
    )(decay, teacher, student, token)


def hold_kernel(value, token, out):
    out[...] = value[...]


def hold(value, token):
    return pl.pallas_call(
        hold_kernel,
        in_specs=[pl.BlockSpec(memory_space=pltpu.VMEM), pl.BlockSpec(memory_space=pl.ANY)],
        out_shape=jax.ShapeDtypeStruct(value.shape, F32),
        compiler_params=params(8),
        cost_estimate=pl.CostEstimate(flops=0, bytes_accessed=10**6, transcendentals=0),
        name="hold",
    )(value, token)


def duo_kernel(own, core, out):
    out[0] = own[...]
    out[1] = core[...]


def duo(own, core):
    return pl.pallas_call(
        duo_kernel,
        out_shape=jax.ShapeDtypeStruct((2, HALF, PACK), F32),
        compiler_params=params(16),
        cost_estimate=pl.CostEstimate(flops=0, bytes_accessed=10**6, transcendentals=0),
        name="duo",
    )(own, core)


CONV_COLS = 4 * GROUP_CH


def conv_kernel(x, left, right, weight, gain, token, mixed, top, bottom, padded, *scratch):
    groups, taps, rhs = scratch[0:2], scratch[2:4], scratch[4:6]
    step = pl.program_id(0)

    @pl.when(step == 0)
    def _():
        for ref in rhs:
            ref[...] = jnp.zeros_like(ref)

    padded[0:REACH, :] = left[...]
    padded[REACH:REACH + ROWS, :] = x[...]
    padded[REACH + ROWS:, :] = right[...]
    outs = []
    for q in range(4):
        cut = slice(q * GROUP_CH, (q + 1) * GROUP_CH)
        group, tap, part = groups[q % 2], taps[q % 2], rhs[q % 2]
        group[...] = jnp.concatenate(
            [padded[:, cut], jnp.zeros((ROWS + 2 * REACH, 128 - GROUP_CH), F32)], axis=1
        )
        for j in range(KERNEL):
            at = j * 128
            high, low = two_terms(group[j:j + ROWS, :])
            tap[0:ROWS, at:at + 128] = high
            tap[ROWS:, at:at + 128] = low
            wide = jnp.concatenate(
                [weight[j, :, cut], jnp.zeros((GROUP_CH, 128 - GROUP_CH), F32)], axis=1
            )
            high, low = two_terms(wide)
            part[at:at + GROUP_CH, 0:128] = high
            part[at:at + GROUP_CH, 128:256] = low
        both = mm(tap[...], part[...])
        both = both[:ROWS] + both[ROWS:]
        outs.append((both[:, :128] + both[:, 128:])[:, :GROUP_CH])
    conv = jnp.concatenate(outs, axis=1)
    value = x[...] + 0.5 * conv * (1.0 + lax.erf(conv * (0.5 ** 0.5)))
    for s in range(D // CONV_COLS):
        @pl.when(step == s)
        def _():
            mixed[:, s * CONV_COLS:(s + 1) * CONV_COLS] = value

    @pl.when(step == D // CONV_COLS - 1)
    def _():
        whole = mixed[...]
        center = jnp.sum(whole, axis=1, keepdims=True) * (1.0 / D)
        shifted = whole - center
        spread = jnp.sum(shifted * shifted, axis=1, keepdims=True) * (1.0 / D)
        normed = shifted * (1.0 / jnp.sqrt(spread + 1e-5)) * gain[...]
        top[...] = normed[:ROWS // 2]
        bottom[...] = normed[ROWS // 2:]


def conv_norm(frames, left, right, weight, gain, token):
    whole = pl.BlockSpec((ROWS, D), lambda i: (0, 0))
    half = pl.BlockSpec((ROWS // 2, D), lambda i: (0, 0))
    edge = pl.BlockSpec((REACH, CONV_COLS), lambda i: (0, i))
    return pl.pallas_call(
        conv_kernel,
        grid=(D // CONV_COLS,),
        in_specs=[
            pl.BlockSpec((ROWS, CONV_COLS), lambda i: (0, i)),
            edge,
            edge,
            pl.BlockSpec((KERNEL, GROUP_CH, CONV_COLS), lambda i: (0, 0, i)),
            pl.BlockSpec((1, D), lambda i: (0, 0)),
            pl.BlockSpec(memory_space=pl.ANY),
        ],
        out_specs=[whole, half, half],
        out_shape=[jax.ShapeDtypeStruct((ROWS, D), F32)] + [jax.ShapeDtypeStruct((ROWS // 2, D), F32)] * 2,
        scratch_shapes=[
            pltpu.VMEM((ROWS + 2 * REACH, CONV_COLS), F32),
        ]
        + [pltpu.VMEM((ROWS + 2 * REACH, 128), F32)] * 2
        + [pltpu.VMEM((2 * ROWS, KERNEL * 128), BF16)] * 2
        + [pltpu.VMEM((KERNEL * 128, 256), BF16)] * 2,
        compiler_params=params(56),
        cost_estimate=pl.CostEstimate(flops=10**6, bytes_accessed=10**6, transcendentals=0),
        name="conv_norm",
    )(frames, left, right, weight, gain, token)


def sort_kernel(place, own, core, cross, *refs):
    high, low, out_part, out_half = refs[-4:]
    dp = place[0]
    parts = (own[...], core[...], cross[0], cross[1])

    def tensor(t):
        which = jnp.bitwise_xor(dp, t)
        return jnp.where(
            which == 0, parts[0], jnp.where(which == 1, parts[1], jnp.where(which == 2, parts[2], parts[3]))
        )

    query, key, value = tensor(0), tensor(1), tensor(2)
    out_part[...] = tensor(3)
    turns = pl.num_programs(0) // 2

    @pl.when(pl.program_id(0) // turns == dp % 2)
    def _():
        out_half[pl.ds(pl.program_id(0) % turns * out_part.shape[0], out_part.shape[0]), :] = out_part[...]

    gap = jnp.zeros((query.shape[0], 256 - COLS), F32)
    for half in range(2):
        cut = slice(half * COLS, (half + 1) * COLS)
        wide = jnp.concatenate([query[:, cut], gap, key[:, cut], value[:, cut]], axis=1)
        high[half], low[half] = two_terms(wide)


def sort_parts(place, own, core, cross):
    step = 96
    block = pl.BlockSpec((step, PACK), lambda i: (i, 0))
    wide = pl.BlockSpec((2, step, 256 + PACK), lambda i: (0, i, 0))
    high, low, out_part, out_half = pl.pallas_call(
        sort_kernel,
        grid=(HALF // step,),
        in_specs=[pl.BlockSpec(memory_space=pltpu.SMEM)]
        + [block] * 2
        + [pl.BlockSpec((2, step, PACK), lambda i: (0, i, 0))],
        out_specs=[wide, wide, block, pl.BlockSpec((HALF // 2, PACK), lambda i: (0, 0))],
        out_shape=[jax.ShapeDtypeStruct((2, HALF, 256 + PACK), BF16)] * 2
        + [jax.ShapeDtypeStruct((HALF, PACK), F32), jax.ShapeDtypeStruct((HALF // 2, PACK), F32)],
        compiler_params=params(24),
        cost_estimate=pl.CostEstimate(flops=10**7, bytes_accessed=10 * MIB, transcendentals=0),
        name="sort_parts",
    )(place, own, core, cross)
    return high.reshape(D, 256 + PACK), low.reshape(D, 256 + PACK), out_part, out_half


def collect_kernel(before, after, far, token, out, sems):
    copies = [
        pltpu.make_async_copy(ref, out.at[n], sems.at[n]) for n, ref in enumerate((before, after, far))
    ]
    for copy in copies:
        copy.start()
    for copy in copies:
        copy.wait()


def collect(*operands):
    anywhere = pl.BlockSpec(memory_space=pl.ANY)
    return pl.pallas_call(
        collect_kernel,
        in_specs=[anywhere] * 4,
        out_specs=anywhere,
        out_shape=jax.ShapeDtypeStruct((QUAD - 1, HALF // 2, PACK), F32),
        scratch_shapes=[pltpu.SemaphoreType.DMA((QUAD - 1,))],
        compiler_params=params(8),
        cost_estimate=pl.CostEstimate(flops=10**6, bytes_accessed=10**6, transcendentals=0),
        name="collect",
    )(*operands)


def split_out_kernel(place, own, mine, other, high, low):
    here = pl.program_id(0) // (pl.num_programs(0) // 2) == place[0] % 2
    for g in range(QUAD):
        whole = own[...] if g == 0 else jnp.where(here, mine[g - 1], other[g - 1])
        for half in range(2):
            high[g, half], low[g, half] = two_terms(whole[:, half * COLS:(half + 1) * COLS])


def split_out(place, own, mine, other):
    step = 192
    turns = HALF // step // 2
    out = pl.BlockSpec((QUAD, 2, step, COLS), lambda i: (0, 0, i, 0))
    part = pl.BlockSpec((QUAD - 1, step, PACK), lambda i: (0, i % turns, 0))
    return pl.pallas_call(
        split_out_kernel,
        grid=(HALF // step,),
        in_specs=[
            pl.BlockSpec(memory_space=pltpu.SMEM),
            pl.BlockSpec((step, PACK), lambda i: (i, 0)),
            part,
            part,
        ],
        out_specs=[out, out],
        out_shape=[jax.ShapeDtypeStruct((QUAD, 2, HALF, COLS), BF16)] * 2,
        compiler_params=params(16),
        cost_estimate=pl.CostEstimate(flops=10**6, bytes_accessed=10**6, transcendentals=0),
        name="split_out",
    )(place, own, mine, other)


SCALE = HEAD_DIM ** (-0.5) * LOG2E
NEAR = 3 * ROWS
FAR = ROWS


def projected(rows, high, low):
    rows_high, rows_low = two_terms(rows)
    return mm(rows_high, high[...]) + mm(rows_high, low[...]) + mm(rows_low, high[...])


def project_cost(rows):
    return pl.CostEstimate(flops=6 * rows * D * 640, bytes_accessed=4 * MIB, transcendentals=0)


def project_near_kernel(*refs):
    high, low, queries, pairs = refs[-4:]
    values = []
    for n in range(3):
        rows = jnp.concatenate([refs[2 * n][...], refs[2 * n + 1][...]], axis=0)
        value = projected(rows, high, low)
        pairs[n * ROWS:(n + 1) * ROWS, :] = value[:, 256:]
        values.append(value[:, :COLS] * SCALE)
    half = ROWS // 2
    first, second, third = values
    queries[0:half, :] = jnp.concatenate([first[:half], second[half:]], axis=1)
    queries[half:ROWS, :] = jnp.concatenate([first[half:], third[:half]], axis=1)
    queries[ROWS:, :] = jnp.concatenate([second[:half], third[half:]], axis=1)


def project_near(*operands):
    return pl.pallas_call(
        project_near_kernel,
        out_shape=[jax.ShapeDtypeStruct((NEAR // 2, PACK), F32), jax.ShapeDtypeStruct((NEAR, PACK), F32)],
        compiler_params=params(24),
        cost_estimate=pl.CostEstimate(flops=6 * NEAR * D * 640, bytes_accessed=40 * MIB, transcendentals=0),
        name="project_near",
    )(*operands)


def project_far_kernel(far_a, far_b, near_queries, near_pairs, high, low, queries, pairs):
    half = ROWS // 2
    value = projected(jnp.concatenate([far_a[...], far_b[...]], axis=0), high, low)
    pairs[0:NEAR, :] = near_pairs[...]
    pairs[NEAR:, :] = value[:, 256:]
    value = value[:, :COLS] * SCALE
    queries[0:NEAR // 2, :] = near_queries[...]
    queries[NEAR // 2:, :] = jnp.concatenate([value[:half], value[half:]], axis=1)


def project_far(*operands):
    return pl.pallas_call(
        project_far_kernel,
        out_shape=[
            jax.ShapeDtypeStruct((SPAN // 2, PACK), F32),
            jax.ShapeDtypeStruct((SPAN, PACK), F32),
        ],
        compiler_params=params(24),
        cost_estimate=project_cost(ROWS),
        name="project_far",
    )(*operands)


def halves_kernel(before, after, token, first, second):
    half = SPAN // 2
    first[...] = after[0:half, :]
    second[...] = before[half:, :]


def halves(*operands):
    vmem = pl.BlockSpec(memory_space=pltpu.VMEM)
    return pl.pallas_call(
        halves_kernel,
        in_specs=[vmem] * 2 + [pl.BlockSpec(memory_space=pl.ANY)],
        out_shape=[jax.ShapeDtypeStruct((SPAN // 2, PACK), F32)] * 2,
        compiler_params=params(12),
        cost_estimate=pl.CostEstimate(flops=10**5, bytes_accessed=2 * MIB, transcendentals=0),
        name="halves",
    )(*operands)


def doubled(tile, odd):
    lane = lax.broadcasted_iota(jnp.int32, tile.shape, 1)
    turned = pltpu.roll(tile, 64, 1)
    return jnp.where((lane < 64) == (odd == 0), tile, turned)


def chunk(ref, c):
    return doubled(ref[:, (c // 2) * 128:(c // 2) * 128 + 128], c % 2)


def attend_kernel(n_queries, n_blocks, state_rows, has_token, *refs):
    refs = list(refs)
    query_refs = [refs.pop(0) for _ in range(n_queries)]
    block_refs = [refs.pop(0) for _ in range(n_blocks)]
    state_refs = [refs.pop(0) for _ in state_rows]
    if has_token:
        refs.pop(0)
    state, query_cat, key_cat, value_cat, even, odd = refs
    at = 0
    for ref in query_refs:
        count = ref.shape[0]
        for half in range(2):
            for h in range(LOCAL_HEADS):
                value = chunk(ref, half * LOCAL_HEADS + h)
                lane = lax.broadcasted_iota(jnp.int32, value.shape, 1)
                high = value.astype(BF16).astype(F32)
                mixture = jnp.where(lane < 64, high, value - high).astype(BF16)
                query_cat[h, at:at + count, 0:128] = mixture
                query_cat[h, at:at + count, 128:256] = mixture
            at += count
    at = 0
    for ref in block_refs:
        count = ref.shape[0]
        for h in range(LOCAL_HEADS):
            high, low = two_terms(chunk(ref, h))
            key_cat[h, at:at + count, 0:128] = high
            key_cat[h, at:at + count, 128:256] = low
            value = chunk(ref, LOCAL_HEADS + h)
            lane = lax.broadcasted_iota(jnp.int32, value.shape, 1)
            high = value.astype(BF16).astype(F32)
            low = value - high
            high = jnp.where(lane < 64, high, jnp.where(lane == L_AT, 1.0, 0.0))
            value_cat[h, at:at + count, 0:128] = high.astype(BF16)
            value_cat[h, at:at + count, 128:256] = jnp.where(lane < 64, low, 0.0).astype(BF16)
        at += count

    at = 0
    for ref, (row, count) in zip(state_refs, state_rows):
        state[:, at:at + count, :] = ref[:, row:row + count, :]
        at += count

    def place(i):
        return i % LOCAL_HEADS, i // LOCAL_HEADS * SPAN

    def scores(i):
        h, at = place(i)
        return mm_nt(query_cat[h, pl.ds(at, SPAN), :], key_cat[h])

    def finish(i, value):
        h, at = place(i)
        top = jnp.max(value, axis=1, keepdims=True)
        if state_rows:
            before = state[h, pl.ds(at, SPAN), :]
            old = before[:, M_AT:M_AT + 1]
            top = jnp.maximum(top, old)
        high, low = two_terms(jnp.exp2(value - top))
        both = mm(jnp.concatenate([high, low], axis=0), value_cat[h])
        both = both[:SPAN] + both[SPAN:]
        after = both[:, :128] + both[:, 128:]
        if state_rows:
            after = after + before * jnp.exp2(old - top)
        lane = lax.broadcasted_iota(jnp.int32, after.shape, 1)
        state[h, pl.ds(at, SPAN), :] = jnp.where(lane == M_AT, top, after)

    total = state.shape[1] // SPAN * LOCAL_HEADS
    even[...] = scores(0)

    def body(j, _):
        i = 2 * j
        odd[...] = scores(i + 1)
        finish(i, even[...])
        even[...] = scores(i + 2)
        finish(i + 1, odd[...])
        return 0

    pairs = (total - 1) // 2
    lax.fori_loop(0, pairs, body, 0)
    if total % 2 == 0:
        odd[...] = scores(total - 1)
        finish(total - 2, even[...])
        finish(total - 1, odd[...])
    else:
        finish(total - 1, even[...])


def attend(queries, blocks, states=(), state_rows=(), token=None, cost=1):
    rows = sum(2 * q.shape[0] for q in queries)
    keys = sum(b.shape[0] for b in blocks)
    shape = jax.ShapeDtypeStruct((LOCAL_HEADS, rows, 128), F32)
    operands = list(queries) + list(blocks) + list(states)
    specs = [pl.BlockSpec(memory_space=pltpu.VMEM)] * len(operands)
    if token is not None:
        operands.append(token)
        specs.append(pl.BlockSpec(memory_space=pl.ANY))
    return pl.pallas_call(
        functools.partial(attend_kernel, len(queries), len(blocks), state_rows, token is not None),
        in_specs=specs,
        out_shape=shape,
        scratch_shapes=[
            pltpu.VMEM((LOCAL_HEADS, rows, 256), BF16),
            pltpu.VMEM((LOCAL_HEADS, keys, 256), BF16),
            pltpu.VMEM((LOCAL_HEADS, keys, 256), BF16),
            pltpu.VMEM((SPAN, keys), F32),
            pltpu.VMEM((SPAN, keys), F32),
        ],
        compiler_params=params({640: 20, 1280: 30}.get(keys, 42)),
        cost_estimate=pl.CostEstimate(flops=cost * 10**6, bytes_accessed=cost * 10**6, transcendentals=0),
        name="attend",
    )(*operands)


def pack_kernel(state, packed):
    first, second, third = state[0], state[1], state[2]
    lane = lax.broadcasted_iota(jnp.int32, first.shape, 1)
    packed[:, 0:128] = jnp.where(lane < 64, first, pltpu.roll(second, 64, 1))
    packed[:, 128:256] = jnp.where(
        lane < 66, third, jnp.where(lane < 68, pltpu.roll(first, 2, 1), pltpu.roll(second, 4, 1))
    )


def pack(state):
    return pl.pallas_call(
        pack_kernel,
        out_shape=jax.ShapeDtypeStruct((SPAN, 256), F32),
        compiler_params=params(16),
        cost_estimate=pl.CostEstimate(flops=10**6, bytes_accessed=2 * MIB, transcendentals=0),
        name="pack",
    )(state)


def merge_kernel(state, packed, own, left, right, far):
    lane = lax.broadcasted_iota(jnp.int32, (SPAN, 128), 1)
    front, back = packed[:, 0:128], packed[:, 128:256]
    theirs = (
        (front, back[:, 66:67], back[:, 67:68]),
        (pltpu.roll(front, 64, 1), back[:, 68:69], back[:, 69:70]),
        (back, back[:, 64:65], back[:, 65:66]),
    )
    heads = []
    for h in range(LOCAL_HEADS):
        mine = state[h]
        other, other_sum, other_top = theirs[h]
        my_sum, my_top = mine[:, L_AT:L_AT + 1], mine[:, M_AT:M_AT + 1]
        top = jnp.maximum(my_top, other_top)
        a, b = jnp.exp2(my_top - top), jnp.exp2(other_top - top)
        share = 1.0 / (my_sum * a + other_sum * b)
        heads.append(mine * (a * share) + other * (b * share))
    tile = jnp.where(lane < 64, heads[0], pltpu.roll(heads[1], 64, 1))
    attended = jnp.concatenate([tile, heads[2][:, :64]], axis=1)
    half = ROWS // 2
    pieces = [attended[n * half:(n + 1) * half] for n in range(2 * QUAD)]
    for ref, (a, b) in ((own, (0, 1)), (left, (2, 4)), (right, (5, 6)), (far, (3, 7))):
        ref[...] = jnp.concatenate([pieces[a], pieces[b]], axis=1)


def merge(state, packed):
    return pl.pallas_call(
        merge_kernel,
        out_shape=[jax.ShapeDtypeStruct((ROWS // 2, PACK), F32)] * 4,
        compiler_params=params(24),
        cost_estimate=pl.CostEstimate(flops=10**6, bytes_accessed=2 * MIB, transcendentals=0),
        name="merge",
    )(state, packed)


def output_kernel(mixed, own, before, after, far, high, low, out):
    terms = [two_terms(jnp.concatenate([ref[:, :COLS], ref[:, COLS:]], axis=0)) for ref in (own, before, after, far)]
    for half in range(2):
        cut = slice(half * HALF, (half + 1) * HALF)
        total = mixed[:, cut]
        for g, (rows_high, rows_low) in enumerate(terms):
            total = total + (
                mm_nt(rows_high, high[g, half])
                + mm_nt(rows_high, low[g, half])
                + mm_nt(rows_low, high[g, half])
            )
        out[:, cut] = total


def output(*operands):
    return pl.pallas_call(
        output_kernel,
        out_shape=jax.ShapeDtypeStruct((ROWS, D), F32),
        compiler_params=params(32),
        cost_estimate=pl.CostEstimate(flops=6 * ROWS * 768 * D, bytes_accessed=8 * MIB, transcendentals=0),
        name="output",
    )(*operands)


def ctx_pairs(dx=0, dy=0, dz=0):
    return [
        ((x * 2 + y) * 4 + z, (((x + dx) % 4) * 2 + (y + dy) % 2) * 4 + (z + dz) % 4)
        for x in range(4)
        for y in range(2)
        for z in range(4)
    ]


def dp_pairs(flip_hi, flip_core):
    pairs = []
    for dp in range(4):
        for ctx in range(32):
            to_dp = dp ^ (2 * flip_hi + flip_core)
            to_ctx = ctx ^ 4 if flip_hi else ctx
            pairs.append((dp * 32 + ctx, to_dp * 32 + to_ctx))
    return pairs


def to_x(value, shift):
    return lax.ppermute(value, "ctx", ctx_pairs(dx=shift))


def to_y(value):
    return lax.ppermute(value, "ctx", ctx_pairs(dy=1))


def to_z(value, shift):
    return lax.ppermute(value, "ctx", ctx_pairs(dz=shift))


def local(frames, teacher, student, decay, conv_weight, norm_gain):
    dp, ctx = lax.axis_index("dp"), lax.axis_index("ctx")
    place = jnp.stack([dp, ctx // 8]).astype(jnp.int32)
    rows = frames[0]
    part, head, tail = head_part(place, decay, rows, teacher, student)
    left = lax.ppermute(tail, "ctx", [(i, i + 1) for i in range(31)])
    right = lax.ppermute(head, "ctx", [(i + 1, i) for i in range(31)])

    core = lax.ppermute(part, ("dp", "ctx"), dp_pairs(0, 1))
    both = duo(part, core)
    cross = lax.ppermute(both, ("dp", "ctx"), dp_pairs(1, 0))

    mixed, top, bottom = conv_norm(rows, left, right, conv_weight, norm_gain.reshape(1, D), both)
    after_top, before_bottom = to_x(top, -1), to_x(bottom, 1)
    far_a, far_b = to_x(after_top, -1), to_x(before_bottom, 1)
    after_bottom, before_top = to_x(bottom, -1), to_x(top, 1)
    refreshed = refresh(decay, teacher, student, top)
    high, low, out_part, out_half = sort_parts(place, part, core, cross)
    near_queries, near_pairs = project_near(
        top, bottom, before_top, before_bottom, after_top, after_bottom, high, low
    )
    mine, pairs = project_far(far_a, far_b, near_queries, near_pairs, high, low)
    partner = to_y(mine)
    around = [to_z(pairs, 1), to_z(pairs, -1)]

    all_rows = (0, SPAN)
    ours = attend([mine], [pairs])
    theirs = attend([partner], [pairs], token=ours)
    out_half = hold(out_half, theirs)
    out_halves = [to_x(out_half, 1), to_x(out_half, -1), to_x(out_half, 2)]
    first, second = halves(*around, theirs)
    opposite = [to_z(first, -1), to_z(second, 1)]
    theirs = attend([partner], around, [theirs], (all_rows,), first, cost=20)
    theirs = attend([partner], opposite, [theirs], (all_rows,))
    sums = pack(theirs)
    packed = to_y(sums)
    ours = attend([mine], around + opposite, [ours], (all_rows,), sums)
    own, to_before, to_after, to_far = merge(ours, packed)
    collected = collect(*out_halves, sums)
    other = lax.ppermute(collected, ("dp", "ctx"), dp_pairs(0, 1))
    out_high, out_low = split_out(place, out_part, collected, other)

    from_after = to_x(to_before, -1)
    from_before = to_x(to_after, 1)
    from_far = to_x(to_far, 2)
    out = output(mixed, own, from_before, from_after, from_far, out_high, out_low)
    return out[None], refreshed


def solution(mesh):
    return jax.shard_map(
        local,
        mesh=mesh,
        in_specs=(
            P("dp", "ctx", None),
            P("dp", None, None),
            P("dp", None, None),
            P("dp"),
            P(),
            P(),
        ),
        out_specs=(P("dp", "ctx", None), P("dp", None, None)),
        check_vma=False,
    )
```

```python
import functools

import jax
import jax.numpy as jnp
from jax import lax
from jax.experimental import pallas as pl
from jax.experimental.pallas import tpu as pltpu
from jax.sharding import PartitionSpec as P

D = 1536
HEADS = 12
HEAD_DIM = 64
GROUP_CH = 96
KERNEL = 16
REACH = KERNEL // 2
ROWS = 160
QUAD = 4
COLS = HEADS * HEAD_DIM // QUAD
LOCAL_HEADS = HEADS // QUAD
HALF = D // 2
PACK = 2 * COLS
SPAN = QUAD * ROWS
LOG2E = 1.4426950408889634
MIB = 1 << 20
F32 = jnp.float32
BF16 = jnp.bfloat16
L_AT = HEAD_DIM
M_AT = HEAD_DIM + 1


def params(mib):
    return pltpu.CompilerParams(vmem_limit_bytes=mib * MIB)


def two_terms(value):
    high = value.astype(BF16)
    return high, (value - high.astype(F32)).astype(BF16)


def mm(a, b):
    return jnp.dot(a, b, preferred_element_type=F32)


def mm_nt(a, b):
    return lax.dot_general(a, b, (((1,), (1,)), ((), ())), preferred_element_type=F32)


WINDOW = 256


PIECES = 4


def part_kernel(place, decay, frames, teacher, student, part, head, tail, old, new, sems):
    start = pl.multiple_of((3 * place[1] // 2) * 128, 128)
    step = HALF // PIECES
    copies = []
    for n, (src, dst) in enumerate(((teacher, old), (student, new))):
        for half in range(2):
            for piece in range(PIECES):
                rows = pl.ds(piece * step, step)
                copies.append(
                    pltpu.make_async_copy(
                        src.at[half, rows, pl.ds(start, WINDOW)], dst.at[half, rows, :], sems.at[n, half, piece]
                    )
                )
    for copy in copies:
        copy.start()
    head[...] = frames[0:REACH, :]
    tail[...] = frames[ROWS - REACH:, :]
    for copy in copies:
        copy.wait()
    rate = decay[0]
    odd = place[1] % 2
    for shift in range(2):
        @pl.when(odd == shift)
        def _():
            cut = slice(shift * 64, shift * 64 + COLS)
            halves = [rate * old[n, :, cut] + (1.0 - rate) * new[n, :, cut] for n in range(2)]
            part[...] = jnp.concatenate(halves, axis=1)


def head_part(place, decay, frames, teacher, student):
    smem = pl.BlockSpec(memory_space=pltpu.SMEM)
    hbm = pl.BlockSpec(memory_space=pltpu.HBM)
    return pl.pallas_call(
        part_kernel,
        in_specs=[smem, smem, pl.BlockSpec(memory_space=pltpu.VMEM), hbm, hbm],
        out_shape=[
            jax.ShapeDtypeStruct((HALF, PACK), F32),
            jax.ShapeDtypeStruct((REACH, D), F32),
            jax.ShapeDtypeStruct((REACH, D), F32),
        ],
        scratch_shapes=[
            pltpu.VMEM((2, HALF, WINDOW), F32),
            pltpu.VMEM((2, HALF, WINDOW), F32),
            pltpu.SemaphoreType.DMA((2, 2, PIECES)),
        ],
        compiler_params=params(56),
        cost_estimate=pl.CostEstimate(flops=4 * D * COLS, bytes_accessed=4 * MIB, transcendentals=0),
        name="head_part",
    )(place, decay, frames, teacher.reshape(2, HALF, 768), student.reshape(2, HALF, 768))


def refresh_kernel(decay, teacher, student, token, refreshed, done):
    done[...] = jnp.zeros_like(done)
    rate = decay[0]
    refreshed[...] = rate * teacher[...] + (1.0 - rate) * student[...]


def refresh(decay, teacher, student, token):
    step = 384
    block = pl.BlockSpec((1, step, 768), lambda i: (0, i, 0))
    return pl.pallas_call(
        refresh_kernel,
        grid=(D // step,),
        in_specs=[pl.BlockSpec(memory_space=pltpu.SMEM), block, block, pl.BlockSpec(memory_space=pl.ANY)],
        out_specs=[block, pl.BlockSpec((8, 128), lambda i: (0, 0))],
        out_shape=[jax.ShapeDtypeStruct((1, D, 768), F32), jax.ShapeDtypeStruct((8, 128), F32)],
        compiler_params=params(16),
        cost_estimate=pl.CostEstimate(flops=4 * D * 768, bytes_accessed=14 * MIB, transcendentals=0),
        name="refresh",
    )(decay, teacher, student, token)


def hold_kernel(value, token, other, out):
    out[...] = value[...]


def hold(value, *tokens):
    return pl.pallas_call(
        hold_kernel,
        in_specs=[pl.BlockSpec(memory_space=pltpu.VMEM)] + [pl.BlockSpec(memory_space=pl.ANY)] * 2,
        out_shape=jax.ShapeDtypeStruct(value.shape, F32),
        compiler_params=params(8),
        cost_estimate=pl.CostEstimate(flops=0, bytes_accessed=10**6, transcendentals=0),
        name="hold",
    )(value, *tokens)


def duo_kernel(own, core, out):
    out[0] = own[...]
    out[1] = core[...]


def duo(own, core):
    return pl.pallas_call(
        duo_kernel,
        out_shape=jax.ShapeDtypeStruct((2, HALF, PACK), F32),
        compiler_params=params(16),
        cost_estimate=pl.CostEstimate(flops=0, bytes_accessed=10**6, transcendentals=0),
        name="duo",
    )(own, core)


CONV_COLS = 4 * GROUP_CH


def conv_kernel(x, left, right, weight, gain, token, mixed, top, bottom, padded, *scratch):
    groups, taps, rhs = scratch[0:2], scratch[2:4], scratch[4:6]
    step = pl.program_id(0)

    @pl.when(step == 0)
    def _():
        for ref in rhs:
            ref[...] = jnp.zeros_like(ref)

    padded[0:REACH, :] = left[...]
    padded[REACH:REACH + ROWS, :] = x[...]
    padded[REACH + ROWS:, :] = right[...]
    outs = []
    for q in range(4):
        cut = slice(q * GROUP_CH, (q + 1) * GROUP_CH)
        group, tap, part = groups[q % 2], taps[q % 2], rhs[q % 2]
        group[...] = jnp.concatenate(
            [padded[:, cut], jnp.zeros((ROWS + 2 * REACH, 128 - GROUP_CH), F32)], axis=1
        )
        for j in range(KERNEL):
            at = j * 128
            high, low = two_terms(group[j:j + ROWS, :])
            tap[0:ROWS, at:at + 128] = high
            tap[ROWS:, at:at + 128] = low
            wide = jnp.concatenate(
                [weight[j, :, cut], jnp.zeros((GROUP_CH, 128 - GROUP_CH), F32)], axis=1
            )
            high, low = two_terms(wide)
            part[at:at + GROUP_CH, 0:128] = high
            part[at:at + GROUP_CH, 128:256] = low
        both = mm(tap[...], part[...])
        both = both[:ROWS] + both[ROWS:]
        outs.append((both[:, :128] + both[:, 128:])[:, :GROUP_CH])
    conv = jnp.concatenate(outs, axis=1)
    value = x[...] + 0.5 * conv * (1.0 + lax.erf(conv * (0.5 ** 0.5)))
    for s in range(D // CONV_COLS):
        @pl.when(step == s)
        def _():
            mixed[:, s * CONV_COLS:(s + 1) * CONV_COLS] = value

    @pl.when(step == D // CONV_COLS - 1)
    def _():
        whole = mixed[...]
        center = jnp.sum(whole, axis=1, keepdims=True) * (1.0 / D)
        shifted = whole - center
        spread = jnp.sum(shifted * shifted, axis=1, keepdims=True) * (1.0 / D)
        normed = shifted * (1.0 / jnp.sqrt(spread + 1e-5)) * gain[...]
        top[...] = normed[:ROWS // 2]
        bottom[...] = normed[ROWS // 2:]


def conv_norm(frames, left, right, weight, gain, token):
    whole = pl.BlockSpec((ROWS, D), lambda i: (0, 0))
    half = pl.BlockSpec((ROWS // 2, D), lambda i: (0, 0))
    edge = pl.BlockSpec((REACH, CONV_COLS), lambda i: (0, i))
    return pl.pallas_call(
        conv_kernel,
        grid=(D // CONV_COLS,),
        in_specs=[
            pl.BlockSpec((ROWS, CONV_COLS), lambda i: (0, i)),
            edge,
            edge,
            pl.BlockSpec((KERNEL, GROUP_CH, CONV_COLS), lambda i: (0, 0, i)),
            pl.BlockSpec((1, D), lambda i: (0, 0)),
            pl.BlockSpec(memory_space=pl.ANY),
        ],
        out_specs=[whole, half, half],
        out_shape=[jax.ShapeDtypeStruct((ROWS, D), F32)] + [jax.ShapeDtypeStruct((ROWS // 2, D), F32)] * 2,
        scratch_shapes=[
            pltpu.VMEM((ROWS + 2 * REACH, CONV_COLS), F32),
        ]
        + [pltpu.VMEM((ROWS + 2 * REACH, 128), F32)] * 2
        + [pltpu.VMEM((2 * ROWS, KERNEL * 128), BF16)] * 2
        + [pltpu.VMEM((KERNEL * 128, 256), BF16)] * 2,
        compiler_params=params(56),
        cost_estimate=pl.CostEstimate(flops=10**6, bytes_accessed=10**6, transcendentals=0),
        name="conv_norm",
    )(frames, left, right, weight, gain, token)


def sort_kernel(place, own, core, cross, *refs):
    high, low, out_part, out_half = refs[-4:]
    dp = place[0]
    parts = (own[...], core[...], cross[0], cross[1])

    def tensor(t):
        which = jnp.bitwise_xor(dp, t)
        return jnp.where(
            which == 0, parts[0], jnp.where(which == 1, parts[1], jnp.where(which == 2, parts[2], parts[3]))
        )

    query, key, value = tensor(0), tensor(1), tensor(2)
    out_part[...] = tensor(3)
    turns = pl.num_programs(0) // 2

    @pl.when(pl.program_id(0) // turns == dp % 2)
    def _():
        out_half[pl.ds(pl.program_id(0) % turns * out_part.shape[0], out_part.shape[0]), :] = out_part[...]

    gap = jnp.zeros((query.shape[0], 256 - COLS), F32)
    for half in range(2):
        cut = slice(half * COLS, (half + 1) * COLS)
        wide = jnp.concatenate([query[:, cut], gap, key[:, cut], value[:, cut]], axis=1)
        high[half], low[half] = two_terms(wide)


def sort_parts(place, own, core, cross):
    step = 96
    block = pl.BlockSpec((step, PACK), lambda i: (i, 0))
    wide = pl.BlockSpec((2, step, 256 + PACK), lambda i: (0, i, 0))
    high, low, out_part, out_half = pl.pallas_call(
        sort_kernel,
        grid=(HALF // step,),
        in_specs=[pl.BlockSpec(memory_space=pltpu.SMEM)]
        + [block] * 2
        + [pl.BlockSpec((2, step, PACK), lambda i: (0, i, 0))],
        out_specs=[wide, wide, block, pl.BlockSpec((HALF // 2, PACK), lambda i: (0, 0))],
        out_shape=[jax.ShapeDtypeStruct((2, HALF, 256 + PACK), BF16)] * 2
        + [jax.ShapeDtypeStruct((HALF, PACK), F32), jax.ShapeDtypeStruct((HALF // 2, PACK), F32)],
        compiler_params=params(24),
        cost_estimate=pl.CostEstimate(flops=10**7, bytes_accessed=10 * MIB, transcendentals=0),
        name="sort_parts",
    )(place, own, core, cross)
    return high.reshape(D, 256 + PACK), low.reshape(D, 256 + PACK), out_part, out_half


def collect_kernel(before, after, far, token, out, sems):
    copies = [
        pltpu.make_async_copy(ref, out.at[n], sems.at[n]) for n, ref in enumerate((before, after, far))
    ]
    for copy in copies:
        copy.start()
    for copy in copies:
        copy.wait()


def collect(*operands):
    anywhere = pl.BlockSpec(memory_space=pl.ANY)
    return pl.pallas_call(
        collect_kernel,
        in_specs=[anywhere] * 4,
        out_specs=anywhere,
        out_shape=jax.ShapeDtypeStruct((QUAD - 1, HALF // 2, PACK), F32),
        scratch_shapes=[pltpu.SemaphoreType.DMA((QUAD - 1,))],
        compiler_params=params(8),
        cost_estimate=pl.CostEstimate(flops=10**6, bytes_accessed=10**6, transcendentals=0),
        name="collect",
    )(*operands)


def split_out_kernel(place, own, mine, other, high, low):
    here = pl.program_id(0) // (pl.num_programs(0) // 2) == place[0] % 2
    for g in range(QUAD):
        whole = own[...] if g == 0 else jnp.where(here, mine[g - 1], other[g - 1])
        for half in range(2):
            high[g, half], low[g, half] = two_terms(whole[:, half * COLS:(half + 1) * COLS])


def split_out(place, own, mine, other):
    step = 192
    turns = HALF // step // 2
    out = pl.BlockSpec((QUAD, 2, step, COLS), lambda i: (0, 0, i, 0))
    part = pl.BlockSpec((QUAD - 1, step, PACK), lambda i: (0, i % turns, 0))
    return pl.pallas_call(
        split_out_kernel,
        grid=(HALF // step,),
        in_specs=[
            pl.BlockSpec(memory_space=pltpu.SMEM),
            pl.BlockSpec((step, PACK), lambda i: (i, 0)),
            part,
            part,
        ],
        out_specs=[out, out],
        out_shape=[jax.ShapeDtypeStruct((QUAD, 2, HALF, COLS), BF16)] * 2,
        compiler_params=params(16),
        cost_estimate=pl.CostEstimate(flops=10**6, bytes_accessed=10**6, transcendentals=0),
        name="split_out",
    )(place, own, mine, other)


SCALE = HEAD_DIM ** (-0.5) * LOG2E
NEAR = 3 * ROWS
FAR = ROWS


def projected(rows, high, low):
    rows_high, rows_low = two_terms(rows)
    return mm(rows_high, high[...]) + mm(rows_high, low[...]) + mm(rows_low, high[...])


def project_cost(rows):
    return pl.CostEstimate(flops=6 * rows * D * 640, bytes_accessed=4 * MIB, transcendentals=0)


def project_near_kernel(*refs):
    high, low, queries, pairs = refs[-4:]
    values = []
    for n in range(3):
        rows = jnp.concatenate([refs[2 * n][...], refs[2 * n + 1][...]], axis=0)
        value = projected(rows, high, low)
        pairs[n * ROWS:(n + 1) * ROWS, :] = value[:, 256:]
        values.append(value[:, :COLS] * SCALE)
    half = ROWS // 2
    first, second, third = values
    queries[0:half, :] = jnp.concatenate([first[:half], second[half:]], axis=1)
    queries[half:ROWS, :] = jnp.concatenate([first[half:], third[:half]], axis=1)
    queries[ROWS:, :] = jnp.concatenate([second[:half], third[half:]], axis=1)


def project_near(*operands):
    return pl.pallas_call(
        project_near_kernel,
        out_shape=[jax.ShapeDtypeStruct((NEAR // 2, PACK), F32), jax.ShapeDtypeStruct((NEAR, PACK), F32)],
        compiler_params=params(24),
        cost_estimate=pl.CostEstimate(flops=6 * NEAR * D * 640, bytes_accessed=40 * MIB, transcendentals=0),
        name="project_near",
    )(*operands)


def project_far_kernel(far_a, far_b, near_queries, near_pairs, high, low, queries, pairs):
    half = ROWS // 2
    value = projected(jnp.concatenate([far_a[...], far_b[...]], axis=0), high, low)
    pairs[0:NEAR, :] = near_pairs[...]
    pairs[NEAR:, :] = value[:, 256:]
    value = value[:, :COLS] * SCALE
    queries[0:NEAR // 2, :] = near_queries[...]
    queries[NEAR // 2:, :] = jnp.concatenate([value[:half], value[half:]], axis=1)


def project_far(*operands):
    return pl.pallas_call(
        project_far_kernel,
        out_shape=[
            jax.ShapeDtypeStruct((SPAN // 2, PACK), F32),
            jax.ShapeDtypeStruct((SPAN, PACK), F32),
        ],
        compiler_params=params(24),
        cost_estimate=project_cost(ROWS),
        name="project_far",
    )(*operands)


def halves_kernel(before, after, token, first, second):
    half = SPAN // 2
    first[...] = after[0:half, :]
    second[...] = before[half:, :]


def halves(*operands):
    vmem = pl.BlockSpec(memory_space=pltpu.VMEM)
    return pl.pallas_call(
        halves_kernel,
        in_specs=[vmem] * 2 + [pl.BlockSpec(memory_space=pl.ANY)],
        out_shape=[jax.ShapeDtypeStruct((SPAN // 2, PACK), F32)] * 2,
        compiler_params=params(12),
        cost_estimate=pl.CostEstimate(flops=10**5, bytes_accessed=2 * MIB, transcendentals=0),
        name="halves",
    )(*operands)


def doubled(tile, odd):
    lane = lax.broadcasted_iota(jnp.int32, tile.shape, 1)
    turned = pltpu.roll(tile, 64, 1)
    return jnp.where((lane < 64) == (odd == 0), tile, turned)


def chunk(ref, c):
    return doubled(ref[:, (c // 2) * 128:(c // 2) * 128 + 128], c % 2)


def attend_kernel(n_queries, n_blocks, state_rows, has_token, *refs):
    refs = list(refs)
    query_refs = [refs.pop(0) for _ in range(n_queries)]
    block_refs = [refs.pop(0) for _ in range(n_blocks)]
    state_refs = [refs.pop(0) for _ in state_rows]
    if has_token:
        refs.pop(0)
    state, query_cat, key_cat, value_cat, even, odd = refs
    at = 0
    for ref in query_refs:
        count = ref.shape[0]
        for half in range(2):
            for h in range(LOCAL_HEADS):
                value = chunk(ref, half * LOCAL_HEADS + h)
                lane = lax.broadcasted_iota(jnp.int32, value.shape, 1)
                high = value.astype(BF16).astype(F32)
                mixture = jnp.where(lane < 64, high, value - high).astype(BF16)
                query_cat[h, at:at + count, 0:128] = mixture
                query_cat[h, at:at + count, 128:256] = mixture
            at += count
    at = 0
    for ref in block_refs:
        count = ref.shape[0]
        for h in range(LOCAL_HEADS):
            high, low = two_terms(chunk(ref, h))
            key_cat[h, at:at + count, 0:128] = high
            key_cat[h, at:at + count, 128:256] = low
            value = chunk(ref, LOCAL_HEADS + h)
            lane = lax.broadcasted_iota(jnp.int32, value.shape, 1)
            high = value.astype(BF16).astype(F32)
            low = value - high
            high = jnp.where(lane < 64, high, jnp.where(lane == L_AT, 1.0, 0.0))
            value_cat[h, at:at + count, 0:128] = high.astype(BF16)
            value_cat[h, at:at + count, 128:256] = jnp.where(lane < 64, low, 0.0).astype(BF16)
        at += count

    at = 0
    for ref, (row, count) in zip(state_refs, state_rows):
        state[:, at:at + count, :] = ref[:, row:row + count, :]
        at += count

    def place(i):
        return i % LOCAL_HEADS, i // LOCAL_HEADS * SPAN

    def scores(i):
        h, at = place(i)
        return mm_nt(query_cat[h, pl.ds(at, SPAN), :], key_cat[h])

    def finish(i, value):
        h, at = place(i)
        top = jnp.max(value, axis=1, keepdims=True)
        if state_rows:
            before = state[h, pl.ds(at, SPAN), :]
            old = before[:, M_AT:M_AT + 1]
            top = jnp.maximum(top, old)
        high, low = two_terms(jnp.exp2(value - top))
        both = mm(jnp.concatenate([high, low], axis=0), value_cat[h])
        both = both[:SPAN] + both[SPAN:]
        after = both[:, :128] + both[:, 128:]
        if state_rows:
            after = after + before * jnp.exp2(old - top)
        lane = lax.broadcasted_iota(jnp.int32, after.shape, 1)
        state[h, pl.ds(at, SPAN), :] = jnp.where(lane == M_AT, top, after)

    total = state.shape[1] // SPAN * LOCAL_HEADS
    even[...] = scores(0)

    def body(j, _):
        i = 2 * j
        odd[...] = scores(i + 1)
        finish(i, even[...])
        even[...] = scores(i + 2)
        finish(i + 1, odd[...])
        return 0

    pairs = (total - 1) // 2
    lax.fori_loop(0, pairs, body, 0)
    if total % 2 == 0:
        odd[...] = scores(total - 1)
        finish(total - 2, even[...])
        finish(total - 1, odd[...])
    else:
        finish(total - 1, even[...])


def attend(queries, blocks, states=(), state_rows=(), token=None, cost=1):
    rows = sum(2 * q.shape[0] for q in queries)
    keys = sum(b.shape[0] for b in blocks)
    shape = jax.ShapeDtypeStruct((LOCAL_HEADS, rows, 128), F32)
    operands = list(queries) + list(blocks) + list(states)
    specs = [pl.BlockSpec(memory_space=pltpu.VMEM)] * len(operands)
    if token is not None:
        operands.append(token)
        specs.append(pl.BlockSpec(memory_space=pl.ANY))
    return pl.pallas_call(
        functools.partial(attend_kernel, len(queries), len(blocks), state_rows, token is not None),
        in_specs=specs,
        out_shape=shape,
        scratch_shapes=[
            pltpu.VMEM((LOCAL_HEADS, rows, 256), BF16),
            pltpu.VMEM((LOCAL_HEADS, keys, 256), BF16),
            pltpu.VMEM((LOCAL_HEADS, keys, 256), BF16),
            pltpu.VMEM((SPAN, keys), F32),
            pltpu.VMEM((SPAN, keys), F32),
        ],
        compiler_params=params({640: 20, 1280: 30}.get(keys, 42)),
        cost_estimate=pl.CostEstimate(flops=cost * 10**6, bytes_accessed=cost * 10**6, transcendentals=0),
        name="attend",
    )(*operands)


def pack_kernel(state, packed):
    first, second, third = state[0], state[1], state[2]
    lane = lax.broadcasted_iota(jnp.int32, first.shape, 1)
    packed[:, 0:128] = jnp.where(lane < 64, first, pltpu.roll(second, 64, 1))
    packed[:, 128:256] = jnp.where(
        lane < 66, third, jnp.where(lane < 68, pltpu.roll(first, 2, 1), pltpu.roll(second, 4, 1))
    )


def pack(state):
    return pl.pallas_call(
        pack_kernel,
        out_shape=jax.ShapeDtypeStruct((SPAN, 256), F32),
        compiler_params=params(16),
        cost_estimate=pl.CostEstimate(flops=10**6, bytes_accessed=2 * MIB, transcendentals=0),
        name="pack",
    )(state)


def merge_kernel(state, packed, own, left, right, far):
    lane = lax.broadcasted_iota(jnp.int32, (SPAN, 128), 1)
    front, back = packed[:, 0:128], packed[:, 128:256]
    theirs = (
        (front, back[:, 66:67], back[:, 67:68]),
        (pltpu.roll(front, 64, 1), back[:, 68:69], back[:, 69:70]),
        (back, back[:, 64:65], back[:, 65:66]),
    )
    heads = []
    for h in range(LOCAL_HEADS):
        mine = state[h]
        other, other_sum, other_top = theirs[h]
        my_sum, my_top = mine[:, L_AT:L_AT + 1], mine[:, M_AT:M_AT + 1]
        top = jnp.maximum(my_top, other_top)
        a, b = jnp.exp2(my_top - top), jnp.exp2(other_top - top)
        share = 1.0 / (my_sum * a + other_sum * b)
        heads.append(mine * (a * share) + other * (b * share))
    tile = jnp.where(lane < 64, heads[0], pltpu.roll(heads[1], 64, 1))
    attended = jnp.concatenate([tile, heads[2][:, :64]], axis=1)
    half = ROWS // 2
    pieces = [attended[n * half:(n + 1) * half] for n in range(2 * QUAD)]
    for ref, (a, b) in ((own, (0, 1)), (left, (2, 4)), (right, (5, 6)), (far, (3, 7))):
        ref[...] = jnp.concatenate([pieces[a], pieces[b]], axis=1)


def merge(state, packed):
    return pl.pallas_call(
        merge_kernel,
        out_shape=[jax.ShapeDtypeStruct((ROWS // 2, PACK), F32)] * 4,
        compiler_params=params(24),
        cost_estimate=pl.CostEstimate(flops=10**6, bytes_accessed=2 * MIB, transcendentals=0),
        name="merge",
    )(state, packed)


def output_kernel(mixed, own, before, after, far, high, low, out):
    terms = [two_terms(jnp.concatenate([ref[:, :COLS], ref[:, COLS:]], axis=0)) for ref in (own, before, after, far)]
    for half in range(2):
        cut = slice(half * HALF, (half + 1) * HALF)
        total = mixed[:, cut]
        for g, (rows_high, rows_low) in enumerate(terms):
            total = total + (
                mm_nt(rows_high, high[g, half])
                + mm_nt(rows_high, low[g, half])
                + mm_nt(rows_low, high[g, half])
            )
        out[:, cut] = total


def output(*operands):
    return pl.pallas_call(
        output_kernel,
        out_shape=jax.ShapeDtypeStruct((ROWS, D), F32),
        compiler_params=params(32),
        cost_estimate=pl.CostEstimate(flops=6 * ROWS * 768 * D, bytes_accessed=8 * MIB, transcendentals=0),
        name="output",
    )(*operands)


def ctx_pairs(dx=0, dy=0, dz=0):
    return [
        ((x * 2 + y) * 4 + z, (((x + dx) % 4) * 2 + (y + dy) % 2) * 4 + (z + dz) % 4)
        for x in range(4)
        for y in range(2)
        for z in range(4)
    ]


def dp_pairs(flip_hi, flip_core):
    pairs = []
    for dp in range(4):
        for ctx in range(32):
            to_dp = dp ^ (2 * flip_hi + flip_core)
            to_ctx = ctx ^ 4 if flip_hi else ctx
            pairs.append((dp * 32 + ctx, to_dp * 32 + to_ctx))
    return pairs


def to_x(value, shift):
    return lax.ppermute(value, "ctx", ctx_pairs(dx=shift))


def to_y(value):
    return lax.ppermute(value, "ctx", ctx_pairs(dy=1))


def to_z(value, shift):
    return lax.ppermute(value, "ctx", ctx_pairs(dz=shift))


def local(frames, teacher, student, decay, conv_weight, norm_gain):
    dp, ctx = lax.axis_index("dp"), lax.axis_index("ctx")
    place = jnp.stack([dp, ctx // 8]).astype(jnp.int32)
    rows = frames[0]
    part, head, tail = head_part(place, decay, rows, teacher, student)
    left = lax.ppermute(tail, "ctx", [(i, i + 1) for i in range(31)])
    right = lax.ppermute(head, "ctx", [(i + 1, i) for i in range(31)])

    core = lax.ppermute(part, ("dp", "ctx"), dp_pairs(0, 1))
    both = duo(part, core)
    cross = lax.ppermute(both, ("dp", "ctx"), dp_pairs(1, 0))

    mixed, top, bottom = conv_norm(rows, left, right, conv_weight, norm_gain.reshape(1, D), both)
    after_top, before_bottom = to_x(top, -1), to_x(bottom, 1)
    far_a, far_b = to_x(after_top, -1), to_x(before_bottom, 1)
    after_bottom, before_top = to_x(bottom, -1), to_x(top, 1)
    refreshed, done = refresh(decay, teacher, student, top)
    high, low, out_part, out_half = sort_parts(place, part, core, cross)
    near_queries, near_pairs = project_near(
        top, bottom, before_top, before_bottom, after_top, after_bottom, high, low
    )
    mine, pairs = project_far(far_a, far_b, near_queries, near_pairs, high, low)
    partner = to_y(mine)
    around = [to_z(pairs, 1), to_z(pairs, -1)]

    all_rows = (0, SPAN)
    ours = attend([mine], [pairs])
    theirs = attend([partner], [pairs], token=ours)
    out_half = hold(out_half, theirs, done)
    out_halves = [to_x(out_half, 1), to_x(out_half, -1), to_x(out_half, 2)]
    first, second = halves(*around, theirs)
    opposite = [to_z(first, -1), to_z(second, 1)]
    theirs = attend([partner], around, [theirs], (all_rows,), first, cost=20)
    theirs = attend([partner], opposite, [theirs], (all_rows,))
    sums = pack(theirs)
    packed = to_y(sums)
    ours = attend([mine], around + opposite, [ours], (all_rows,), sums)
    own, to_before, to_after, to_far = merge(ours, packed)
    collected = collect(*out_halves, sums)
    other = lax.ppermute(collected, ("dp", "ctx"), dp_pairs(0, 1))
    out_high, out_low = split_out(place, out_part, collected, other)

    from_after = to_x(to_before, -1)
    from_before = to_x(to_after, 1)
    from_far = to_x(to_far, 2)
    out = output(mixed, own, from_before, from_after, from_far, out_high, out_low)
    return out[None], refreshed


def solution(mesh):
    return jax.shard_map(
        local,
        mesh=mesh,
        in_specs=(
            P("dp", "ctx", None),
            P("dp", None, None),
            P("dp", None, None),
            P("dp"),
            P(),
            P(),
        ),
        out_specs=(P("dp", "ctx", None), P("dp", None, None)),
        check_vma=False,
    )
```
